128 devices in a mesh: gx: 8 (over x, z_lo), gy: 16 (over z_hi, y, core).
Axes of the slice: x: 4, y: 4, z: 4 (z_hi: 2, z_lo: 2; z = z_hi * 2 + z_lo), core: 2. Of those that a mesh axis runs over, the one named last changes fastest.
Arguments:
- tangents: float32 [5, 3, 32, 64, 2048], P(None, None, 'gx', None, 'gy'), may hold values from -72 to 72, as said below
- base_flow: float32 [2, 3, 32, 64, 2048], P(None, None, 'gx', None, 'gy'), may hold values from -4 to 4
- objective_weight: float32 [3, 32, 64, 2048], P(None, 'gx', None, 'gy'), may hold values from -5.6 to 5.6, as said below
Outputs:
- renormed: float32 [5, 3, 32, 64, 2048], P(None, None, 'gx', None, 'gy')
- rfactor: float32 [4, 4], replicated
- coefficients: float32 [4], replicated
- objective: float32 [5], replicated
The draws below stay inside these ranges and needn't reach their ends.
Inputs may be any that keep to these rules, and one draw needn't show every extreme that they name: `tangents`: finite tangent velocities. `objective_weight`: finite weights.
All inputs are finite; a program needn't handle non-finite values.
Results may differ from the reference program's by a relative error of at most 0.000077.
Values sent between devices are 32-bit elements; how exact they have to be, the bound alone decides.
No kernel may reach another device: no remote copies, remote signals or barrier semaphores. Data moves between devices by JAX's collectives and lax.ppermute only.
A program may use at most 128 MiB of HBM per device.

```python
import jax
import jax.numpy as jnp
from jax import lax

NZ = 64
NX = 32
NY = 2048


def random_part(key, salt, dims):
    return jax.random.truncated_normal(jax.random.fold_in(key, salt), -4.0, 4.0, dims, jnp.float32)


def draw_tangents(key, part):
    common = random_part(key, 7, (3, NX, NZ, NY))
    own_part = random_part(key, 17, (5, 3, NX, NZ, NY))
    weights = jax.random.uniform(jax.random.fold_in(key, 13), (5, 1, 1, 1, 1), jnp.float32, 0.5, 1.0)
    along_x = jnp.arange(NX, dtype=jnp.float32) / NX
    along_y = jnp.arange(NY, dtype=jnp.float32) / NY
    profile = jnp.exp(jnp.log(3.0) * along_x)[:, None, None] * jnp.exp(jnp.log(3.0) * along_y)[None, None, :]
    return profile * (weights * common[None] + own_part)


def draw_objective_weight(key, part):
    common = random_part(key, 7, (3, NX, NZ, NY))
    own_part = random_part(key, 23, (3, NX, NZ, NY))
    return 0.6 * common + 0.8 * own_part


def level_of(own_key, extent, split, low, high):
    def one(axis_at, shards_of):
        draws = jax.random.uniform(jax.random.fold_in(jax.random.fold_in(own_key, 6), axis_at), (shards_of,), jnp.float32, low / len(split), high / len(split))
        return jnp.repeat(jnp.exp(draws), extent[axis_at] // shards_of).reshape((-1,) + (1,) * (len(extent) - axis_at - 1))

    level = one(*split[0])
    for cut in split[1:]:
        level = level * one(*cut)
    return level


def centred(stream_key, shape, width, reach, split=(), kind=jnp.bfloat16):
    result = jax.random.normal(stream_key, shape, jnp.float32) * width
    if len(split) > 0:
        result = level_of(stream_key, shape, split, -0.22, 0.18) * result
    return jnp.clip(result, min=-reach, max=reach).astype(kind)


def setup_inputs(seed: int = 0) -> dict:
    key_list = jax.random.split(jax.random.key(seed), 4)
    return {
        "tangents": draw_tangents(jax.random.fold_in(key_list[3], 71), 0),
        "base_flow": centred(key_list[1], (2, 3, NX, NZ, NY), 1.0, 4.0, ((2, 8), (4, 16)), jnp.float32),
        "objective_weight": draw_objective_weight(jax.random.fold_in(key_list[3], 71), 0),
    }


time_step = 0.2
viscosity = 0.05

def neighbour(values_in, step_x, step_y, step_z):
    if step_z != 0:
        padded = jnp.pad(values_in, [(0, 0)] * (values_in.ndim - 2) + [(1, 1), (0, 0)])
        values_in = padded[..., 1 + step_z:1 + step_z + values_in.shape[-2], :]
    return jnp.roll(jnp.roll(values_in, -step_x, axis=-3), -step_y, axis=-1)

def gradients(values_in):
    return (0.5 * (neighbour(values_in, 1, 0, 0) - neighbour(values_in, -1, 0, 0)), 0.5 * (neighbour(values_in, 0, 1, 0) - neighbour(values_in, 0, -1, 0)), 0.5 * (neighbour(values_in, 0, 0, 1) - neighbour(values_in, 0, 0, -1)))

def laplacian(values_in):
    summed = neighbour(values_in, 1, 0, 0) + neighbour(values_in, -1, 0, 0)
    summed = summed + neighbour(values_in, 0, 1, 0) + neighbour(values_in, 0, -1, 0)
    summed = summed + neighbour(values_in, 0, 0, 1) + neighbour(values_in, 0, 0, -1)
    return summed - 6.0 * values_in

def rate_one(fields, flow_in, source_flag):
    field_grad = gradients(fields)
    flow_grad = gradients(flow_in)
    advect = flow_in[0] * field_grad[0] + flow_in[1] * field_grad[1] + flow_in[2] * field_grad[2]
    produce = fields[0] * flow_grad[0] + fields[1] * flow_grad[1] + fields[2] * flow_grad[2]
    return -advect - produce + viscosity * laplacian(fields) + source_flag * laplacian(flow_in)

def lower_inverse(lower_factor):
    count_rows = lower_factor.shape[0]
    identity_rows = jnp.eye(count_rows, dtype=lower_factor.dtype)
    inverse_rows = []
    for row_index in range(count_rows):
        row_value = identity_rows[row_index]
        for column in range(row_index):
            row_value = row_value - lower_factor[row_index, column] * inverse_rows[column]
        inverse_rows.append(row_value / lower_factor[row_index, row_index])
    return jnp.stack(inverse_rows)

def reference(tangents, base_flow, objective_weight):
    highest = lax.Precision.HIGHEST
    flags = (jnp.arange(5) == 4).astype(jnp.float32)

    def advance(pair_in):
        fields, source_flag = pair_in
        first = fields + time_step * rate_one(fields, base_flow[0], source_flag)
        second = 0.5 * (fields + first + time_step * rate_one(first, base_flow[1], source_flag))
        return (second, jnp.sum(objective_weight * first), jnp.sum(objective_weight * second))
    advanced, first_sums, second_sums = lax.map(advance, (tangents, flags))
    total_cells = NX * NY * NZ
    objective = 0.5 * (first_sums + second_sums) / total_cells
    matrix = advanced.reshape(5, -1)
    gram_matrix = jnp.dot(matrix, matrix.T, precision=highest) / (3.0 * total_cells)
    lower_factor = jnp.linalg.cholesky(gram_matrix[:4, :4])
    inverse = lower_inverse(lower_factor)
    coefficients = jnp.dot(inverse, gram_matrix[:4, 4], precision=highest)
    ortho = jnp.dot(inverse, matrix[:4], precision=highest)
    last_row = matrix[4] - jnp.dot(coefficients, ortho, precision=highest)
    renormed = jnp.concatenate([ortho, last_row[None]], 0).reshape(tangents.shape)
    return (renormed, lower_factor.T, coefficients, objective)
```

```python
import functools

import jax
import jax.numpy as jnp
from jax import lax
from jax.experimental import pallas as pl
from jax.experimental.pallas import tpu as pltpu
from jax.sharding import PartitionSpec as P

time_step = 0.2
viscosity = 0.05

groups = ((0, 1, 2), (3, 4))

f32 = jnp.float32
vmem = pl.BlockSpec(memory_space=pltpu.VMEM)
tile = (8, 128)


def shaped(*dims):
    return jax.ShapeDtypeStruct(dims, f32)


def call(body, outs, args, scratch=(), flops=1000000, limit=24):
    return pl.pallas_call(
        body,
        out_shape=outs,
        in_specs=[vmem] * len(args),
        out_specs=jax.tree.map(lambda _: vmem, outs),
        scratch_shapes=list(scratch),
        compiler_params=pltpu.CompilerParams(vmem_limit_bytes=limit << 20),
        cost_estimate=pl.CostEstimate(flops=flops, bytes_accessed=4000000, transcendentals=0),
    )(*args)


def lanes():
    return lax.broadcasted_iota(jnp.int32, tile, 1)


def rows_of(zt):
    return pl.ds(pl.multiple_of(zt * 8, 8), 8)


def sides():
    even = lax.rem(lax.axis_index("gx"), 2) == 0
    z_plane = jnp.where(even, 3, 0)
    z_sign = jnp.where(even, f32(-1), f32(1))
    return ((z_plane, z_sign), (3 - z_plane, -z_sign))


def gy_even():
    return lax.rem(lax.axis_index("gy"), 2) == 0


def column(values, lane):
    return jnp.broadcast_to(values[:, lane : lane + 1], tile)


def faces_kernel(t, u, *outs):
    (z_plane, _), (x_plane, _) = sides()
    last = len(groups) - 1
    for g, members in enumerate(groups):
        sources = [(t, 3 * k + i) for k in members for i in range(3)]
        sources += [(u, i) for i in range(3)] if g == 0 else []
        sources += [(u, 3 + i) for i in range(3)] if g == last else []
        for j, (ref, field) in enumerate(sources):
            outs[2 * g][j] = ref[field, z_plane]
            outs[2 * g + 1][j] = ref[field, x_plane]


def pack_columns(load, count, inner, outer):
    even = gy_even()
    lane = lanes()

    def at_rows(zt, carry):
        rows = rows_of(zt)

        def at_plane(x, packed):
            low, high = packed
            for f in range(count):
                values = load(f, x, rows)
                here = lane == x * 32 + f
                low = jnp.where(here, column(values, 0), low)
                high = jnp.where(here, column(values, 127), high)
            return low, high

        low, high = lax.fori_loop(0, 4, at_plane, (jnp.zeros(tile, f32), jnp.zeros(tile, f32)))
        inner[rows] = jnp.where(even, high, low)
        outer[rows] = jnp.where(even, low, high)
        return carry

    lax.fori_loop(0, 8, at_rows, 0)


def pack_first_kernel(t, u, inner, outer):
    def load(f, x, rows):
        return t[f, x, rows] if f < 15 else u[f - 15, x, rows]

    pack_columns(load, 21, inner, outer)


def fill_padding(padded):
    for f in range(18):
        padded[f, 0] = jnp.zeros((80, 128), f32)
        padded[f, 5] = jnp.zeros((80, 128), f32)

        def at_plane(x, carry):
            padded[f, x, 0:8] = jnp.zeros(tile, f32)
            padded[f, x, 72:80] = jnp.zeros(tile, f32)
            return carry

        lax.fori_loop(1, 5, at_plane, 0)


def section(padded, columns, flow_lane, scale, base, extra, store):
    even = gy_even()
    lane = lanes()
    at_low, at_high = lane == 0, lane == 127

    def at_plane(x, carry):
        for zt in range(8):
            first_row = 8 + 8 * zt
            rows = slice(8 * zt, 8 * zt + 8)
            turn = lax.rem(128 - 32 * x, 128)
            inner, outer = columns[0][rows], columns[1][rows]
            high_side = pltpu.roll(jnp.where(even, inner, outer), turn, axis=1)
            low_side = pltpu.roll(jnp.where(even, outer, inner), turn, axis=1)

            def stencil(f, at):
                def load(dx, dz):
                    return padded[f, x + 1 + dx, first_row + dz : first_row + dz + 8]

                centre = load(0, 0)
                up = jnp.where(at_high, column(high_side, at), pltpu.roll(centre, 127, axis=1))
                down = jnp.where(at_low, column(low_side, at), pltpu.roll(centre, 1, axis=1))
                return centre, load(1, 0), load(-1, 0), up, down, load(0, 1), load(0, -1)

            speed, made, bulk = [], [], []
            for i in range(3):
                flow = stencil(15 + i, flow_lane + i)
                speed.append(flow[0])
                made.append([(-0.5 * scale) * (flow[1 + 2 * j] - flow[2 + 2 * j]) for j in range(3)])
                total = flow[1] + flow[2] + flow[3] + flow[4] + flow[5] + flow[6]
                bulk.append(scale * (total - 6.0 * flow[0]))
            halves = [(0.5 * scale) * u for u in speed]
            ahead = [scale * viscosity - h for h in halves]
            behind = [scale * viscosity + h for h in halves]
            for k in range(5):
                around = [stencil(3 * k + i, 3 * k + i) for i in range(3)]
                for i in range(3):
                    own = around[i]
                    value = (base - 6.0 * viscosity * scale) * own[0]
                    for j in range(3):
                        value += ahead[j] * own[1 + 2 * j] + behind[j] * own[2 + 2 * j]
                        value += made[i][j] * around[j][0]
                    if k == 4:
                        value += bulk[i]
                    if extra is not None:
                        value += 0.5 * extra[3 * k + i, x, rows]
                    store(3 * k + i, x, rows, value)
        return carry

    lax.fori_loop(0, 4, at_plane, 0)


def first_kernel(t, u, inner, outer, *rest):
    outs, padded = rest[:-1], rest[-1]
    fill_padding(padded)

    def copy_plane(x, carry):
        for f in range(15):
            padded[f, x + 1, 8:72] = t[f, x]
        for i in range(3):
            padded[15 + i, x + 1, 8:72] = u[i, x]
        return carry

    lax.fori_loop(0, 4, copy_plane, 0)
    place = {k: (g, n) for g, members in enumerate(groups) for n, k in enumerate(members)}

    def store(f, x, rows, value):
        g, n = place[f // 3]
        outs[g][3 * n + f % 3, x, rows] = value

    section(padded, (inner, outer), 15, time_step, 1.0, None, store)


def halo_terms(scale, sign, speed, tangent, flow_halo):
    weight = scale * viscosity + (0.5 * scale) * sign * speed
    return weight, [
        (0.5 * scale) * sign * v + (scale if k == 4 else 0.0) for k, v in tangent
    ]


def first_faces_kernel(g, part, t, u, z_in, x_in, z_flow, x_flow, z_out, x_out):
    members = groups[g]
    flow_at = 3 * len(groups[0])
    for (plane, sign), got, flow_got, out in zip(sides(), (z_in, x_in), (z_flow, x_flow), (z_out, x_out)):

        def at_rows(zt, carry):
            rows = rows_of(zt)
            flow_halo = [flow_got[flow_at + i, rows] for i in range(3)]
            speed = u[0, plane, rows]
            tangent = [(k, t[3 * k, plane, rows]) for k in members]
            weight, made = halo_terms(time_step, sign, speed, tangent, flow_halo)
            for n in range(len(members)):
                for i in range(3):
                    j = 3 * n + i
                    out[j, rows] = part[j, plane, rows] + weight * got[j, rows] + made[n] * flow_halo[i]
            return carry

        lax.fori_loop(0, 8, at_rows, 0)


def split_refs(refs, *counts):
    pieces, at = [], 0
    for count in counts:
        pieces.append(refs[at : at + count])
        at += count
    pieces.append(refs[at:])
    return pieces


def whole_first(parts, z_faces, x_faces, first):
    (z_plane, _), (x_plane, _) = sides()
    for g, members in enumerate(groups):
        for n, k in enumerate(members):
            for i in range(3):
                f, j = 3 * k + i, 3 * n + i
                first(f, 1, parts[g][j, 1])
                first(f, 2, parts[g][j, 2])
                first(f, z_plane, z_faces[g][j])
                first(f, x_plane, x_faces[g][j])


def pack_second_kernel(*refs):
    count = len(groups)
    parts, z_faces, x_faces, rest = split_refs(refs, count, count, count)
    inner, outer, held = rest

    def put(f, x, values):
        held[f, x] = values

    whole_first(parts, z_faces, x_faces, put)
    pack_columns(lambda f, x, rows: held[f, x, rows], 15, inner, outer)


pairs = [(a, b) for a in range(5) for b in range(a, 5)]


def add_products(sums, rows_now, weighted):
    products = [sums[n] + rows_now[a] * rows_now[b] for n, (a, b) in enumerate(pairs)]
    return products + [sums[15 + k] + weighted[k] for k in range(5)]


def second_kernel(*refs):
    count = len(groups)
    (t, u, weight, flow_inner, flow_outer, inner, outer), parts, z_faces, x_faces, rest = split_refs(
        refs, 7, count, count, count
    )
    out, sums_out, padded, columns_in, columns_out = rest
    fill_padding(padded)

    def put(f, x, values):
        padded[f, x + 1, 8:72] = values

    whole_first(parts, z_faces, x_faces, put)

    def copy_plane(x, carry):
        for i in range(3):
            padded[15 + i, x + 1, 8:72] = u[3 + i, x]
        return carry

    lax.fori_loop(0, 4, copy_plane, 0)
    of_flow = lax.rem(lax.broadcasted_iota(jnp.int32, (64, 128), 1), 32) >= 15
    columns_in[...] = jnp.where(of_flow, flow_inner[...], inner[...])
    columns_out[...] = jnp.where(of_flow, flow_outer[...], outer[...])

    def store(f, x, rows, value):
        out[f, x, rows] = value

    section(padded, (columns_in, columns_out), 18, 0.5 * time_step, 0.5, t, store)

    sums = [jnp.zeros(tile, f32)] * 20
    for x in (1, 2):
        for i in range(3):

            def at_rows(zt, sums):
                rows = rows_of(zt)
                held = pl.ds(pl.multiple_of(zt * 8, 8) + 8, 8)
                now = [out[3 * k + i, x, rows] for k in range(5)]
                scaled = weight[i, x, rows]
                weighted = [scaled * (padded[3 * k + i, x + 1, held] + now[k]) for k in range(5)]
                return add_products(sums, now, weighted)

            sums = lax.fori_loop(0, 8, at_rows, sums)
    for n in range(20):
        sums_out[n] = sums[n]


def second_faces_kernel(*refs):
    count = len(groups)
    (part, u, weight, sums_in, z_flow, x_flow), z_first, x_first, z_in, x_in, rest = split_refs(
        refs, 6, count, count, count, count
    )
    z_out, x_out, sums_out = rest
    last = len(groups) - 1
    flow_at = 3 * len(groups[last]) + (3 if last == 0 else 0)
    scale = 0.5 * time_step
    sums = [sums_in[n] for n in range(20)]
    place = {k: (g, n) for g, members in enumerate(groups) for n, k in enumerate(members)}
    for (plane, sign), first, got, flow_got, out in zip(
        sides(), (z_first, x_first), (z_in, x_in), (z_flow, x_flow), (z_out, x_out)
    ):

        def at_rows(zt, sums):
            rows = rows_of(zt)
            flow_halo = [flow_got[flow_at + i, rows] for i in range(3)]
            speed = u[3, plane, rows]
            tangent = [(k, first[place[k][0]][3 * place[k][1], rows]) for k in range(5)]
            outer_weight, made = halo_terms(scale, sign, speed, tangent, flow_halo)
            for i in range(3):
                now, weighted = [], []
                scaled = weight[i, plane, rows]
                for k in range(5):
                    g, n = place[k]
                    j = 3 * n + i
                    value = part[3 * k + i, plane, rows] + outer_weight * got[g][j, rows] + made[k] * flow_halo[i]
                    out[3 * k + i, rows] = value
                    now.append(value)
                    weighted.append(scaled * (first[g][j, rows] + value))
                sums = add_products(sums, now, weighted)
            return sums

        sums = lax.fori_loop(0, 8, at_rows, sums)
    stacked = jnp.concatenate([jnp.sum(s, axis=0, keepdims=True) for s in sums] + [jnp.zeros((4, 128), f32)], 0)
    totals = jnp.broadcast_to(jnp.sum(stacked, axis=1, keepdims=True), (24, 128))
    diagonal = lax.broadcasted_iota(jnp.int32, (24, 128), 0) == lax.broadcasted_iota(jnp.int32, (24, 128), 1)
    line = jnp.sum(jnp.where(diagonal, totals, 0.0), axis=0, keepdims=True)
    sums_out[...] = jnp.broadcast_to(line[None], sums_out.shape)


def renorm_kernel(total_cells, part, z_faces, x_faces, gathered, out, r_out, c_out, o_out):
    line = jnp.sum(gathered[...], axis=0)
    spread = [jnp.broadcast_to(line[:, n : n + 1], tile) for n in range(20)]
    gram = {pair: spread[n] * f32(1.0 / (3.0 * total_cells)) for n, pair in enumerate(pairs)}
    lower = {}
    for c in range(4):
        value = gram[(c, c)]
        for m in range(c):
            value = value - lower[(c, m)] * lower[(c, m)]
        lower[(c, c)] = jnp.sqrt(value)
        for r in range(c + 1, 4):
            value = gram[(c, r)]
            for m in range(c):
                value = value - lower[(r, m)] * lower[(c, m)]
            lower[(r, c)] = value / lower[(c, c)]
    inverse = {}
    for r in range(4):
        for c in range(r + 1):
            value = jnp.ones(tile, f32) if r == c else jnp.zeros(tile, f32)
            for m in range(c, r):
                value = value - lower[(r, m)] * inverse[(m, c)]
            inverse[(r, c)] = value / lower[(r, r)]
    coefficient = []
    for r in range(4):
        value = inverse[(r, 0)] * gram[(0, 4)]
        for c in range(1, r + 1):
            value = value + inverse[(r, c)] * gram[(c, 4)]
        coefficient.append(value)

    row, lane = lax.broadcasted_iota(jnp.int32, tile, 0), lanes()
    factor, coefficients, objective = (jnp.zeros(tile, f32) for _ in range(3))
    for r in range(4):
        for c in range(r + 1):
            factor = jnp.where((row == c) & (lane == r), lower[(r, c)], factor)
        coefficients = jnp.where(lane == r, coefficient[r], coefficients)
    for k in range(5):
        objective = jnp.where(lane == k, spread[15 + k] * f32(0.5 / total_cells), objective)
    r_out[...] = factor[:4, :4]
    c_out[...] = coefficients[0, :4]
    o_out[...] = objective[0, :5]

    def combine(load, store):
        def at_rows(zt, carry):
            rows = rows_of(zt)
            for i in range(3):
                now = [load(3 * k + i, rows) for k in range(5)]
                last = now[4]
                for r in range(4):
                    value = inverse[(r, 0)] * now[0]
                    for c in range(1, r + 1):
                        value = value + inverse[(r, c)] * now[c]
                    store(3 * r + i, rows, value)
                    last = last - coefficient[r] * value
                store(12 + i, rows, last)
            return carry

        lax.fori_loop(0, 8, at_rows, 0)

    (z_plane, _), (x_plane, _) = sides()
    for plane, load in (
        (1, lambda f, rows: part[f, 1, rows]),
        (2, lambda f, rows: part[f, 2, rows]),
        (z_plane, lambda f, rows: z_faces[f, rows]),
        (x_plane, lambda f, rows: x_faces[f, rows]),
    ):

        def store(f, rows, value):
            out[f, plane, rows] = value

        combine(load, store)


def per_device(tangents, base_flow, objective_weight):
    count_x, count_y = lax.axis_size("gx"), lax.axis_size("gy")
    total_cells = 4 * 64 * 128 * count_x * count_y
    t = tangents.reshape(15, 4, 64, 128)
    u = base_flow.reshape(6, 4, 64, 128)
    last = len(groups) - 1

    def partner(values, axis, count):
        return lax.ppermute(values, axis, [(i, i ^ 1) for i in range(count)])

    def beyond(values, axis, count):
        return lax.ppermute(values, axis, [(i, (i + 2 * (i % 2) - 1) % count) for i in range(count)])

    sizes = [3 * len(members) for members in groups]
    sent = [s + (3 if g == 0 else 0) + (3 if g == last else 0) for g, s in enumerate(sizes)]
    faces = call(faces_kernel, tuple(shaped(s, 64, 128) for s in sent for _ in range(2)), (t, u))
    z_in = [partner(faces[2 * g], "gx", count_x) for g in range(len(groups))]
    x_in = [beyond(faces[2 * g + 1], "gx", count_x) for g in range(len(groups))]
    inner, outer = call(pack_first_kernel, (shaped(64, 128), shaped(64, 128)), (t, u))
    flow_inner = partner(inner, "gy", count_y)
    flow_outer = beyond(outer, "gy", count_y)
    parts = call(
        first_kernel,
        tuple(shaped(s, 4, 64, 128) for s in sizes),
        (t, u, flow_inner, flow_outer),
        scratch=[pltpu.VMEM((18, 6, 80, 128), f32)],
        flops=10000000,
    )
    z_first, x_first, z_next, x_next = [], [], [], []
    for g in range(len(groups)):
        z_face, x_face = call(
            functools.partial(first_faces_kernel, g),
            (shaped(sizes[g], 64, 128), shaped(sizes[g], 64, 128)),
            (parts[g], t, u, z_in[g], x_in[g], z_in[0], x_in[0]),
        )
        z_first.append(z_face)
        x_first.append(x_face)
        z_next.append(partner(z_face, "gx", count_x))
        x_next.append(beyond(x_face, "gx", count_x))
    inner, outer = call(
        pack_second_kernel,
        (shaped(64, 128), shaped(64, 128)),
        (*parts, *z_first, *x_first),
        scratch=[pltpu.VMEM((15, 4, 64, 128), f32)],
    )
    inner = partner(inner, "gy", count_y)
    outer = beyond(outer, "gy", count_y)
    part, sums = call(
        second_kernel,
        (shaped(15, 4, 64, 128), shaped(20, 8, 128)),
        (t, u, objective_weight, flow_inner, flow_outer, inner, outer, *parts, *z_first, *x_first),
        scratch=[
            pltpu.VMEM((18, 6, 80, 128), f32),
            pltpu.VMEM((64, 128), f32),
            pltpu.VMEM((64, 128), f32),
        ],
        flops=10000000,
    )
    z_second, x_second, line = call(
        second_faces_kernel,
        (shaped(15, 64, 128), shaped(15, 64, 128), shaped(count_x * count_y, 1, 128)),
        (part, u, objective_weight, sums, z_in[last], x_in[last], *z_first, *x_first, *z_next, *x_next),
    )
    gathered = lax.all_to_all(line, ("gx", "gy"), 0, 0, tiled=True)
    renormed, rfactor, coefficients, objective = call(
        functools.partial(renorm_kernel, total_cells),
        (shaped(15, 4, 64, 128), shaped(4, 4), shaped(4), shaped(5)),
        (part, z_second, x_second, gathered),
    )
    return (renormed.reshape(tangents.shape), rfactor, coefficients, objective)


def solution(mesh):
    placed = (
        P(None, None, "gx", None, "gy"),
        P(None, None, "gx", None, "gy"),
        P(None, "gx", None, "gy"),
    )
    return jax.shard_map(
        per_device,
        mesh=mesh,
        in_specs=placed,
        out_specs=(P(None, None, "gx", None, "gy"), P(), P(), P()),
        check_vma=False,
    )
```

```python
import functools

import jax
import jax.numpy as jnp
from jax import lax
from jax.experimental import pallas as pl
from jax.experimental.pallas import tpu as pltpu
from jax.sharding import PartitionSpec as P

time_step = 0.2
viscosity = 0.05

groups = ((0, 1, 2), (3, 4))

f32 = jnp.float32
vmem = pl.BlockSpec(memory_space=pltpu.VMEM)
tile = (8, 128)


def shaped(*dims):
    return jax.ShapeDtypeStruct(dims, f32)


def call(body, outs, args, scratch=(), flops=1000000, limit=24):
    return pl.pallas_call(
        body,
        out_shape=outs,
        in_specs=[vmem] * len(args),
        out_specs=jax.tree.map(lambda _: vmem, outs),
        scratch_shapes=list(scratch),
        compiler_params=pltpu.CompilerParams(vmem_limit_bytes=limit << 20),
        cost_estimate=pl.CostEstimate(flops=flops, bytes_accessed=4000000, transcendentals=0),
    )(*args)


def lanes():
    return lax.broadcasted_iota(jnp.int32, tile, 1)


def rows_of(zt):
    return pl.ds(pl.multiple_of(zt * 8, 8), 8)


def sides():
    even = lax.rem(lax.axis_index("gx"), 2) == 0
    z_plane = jnp.where(even, 3, 0)
    z_sign = jnp.where(even, f32(-1), f32(1))
    return ((z_plane, z_sign), (3 - z_plane, -z_sign))


def gy_even():
    return lax.rem(lax.axis_index("gy"), 2) == 0


def faces_kernel(t, u, *refs):
    outs, sem = refs[:-1], refs[-1]
    (z_plane, _), (x_plane, _) = sides()
    last = len(groups) - 1
    copies = []
    for g, members in enumerate(groups):
        sources = [(t, 3 * members[0], 3 * len(members))]
        sources += [(u, 0, 3)] if g == 0 else []
        sources += [(u, 3, 3)] if g == last else []
        for side, plane in ((0, z_plane), (1, x_plane)):
            at = 0
            for ref, start, count in sources:
                copies.append(
                    pltpu.make_async_copy(
                        ref.at[pl.ds(start, count), plane],
                        outs[2 * g + side].at[pl.ds(at, count)],
                        sem.at[len(copies)],
                    )
                )
                at += count
    for copy in copies:
        copy.start()
    for copy in copies:
        copy.wait()


def pack_tile(load, fields, x, packed, even_lane, plane_lane):
    own = jnp.zeros(tile, f32)
    for f in fields:
        own = jnp.where(even_lane == 2 * f, pltpu.roll(load(f), 2 * f + 1, axis=1), own)
    return jnp.where(plane_lane == x, pltpu.roll(own, 32 * x, axis=1), packed)


def lane_parts():
    lane = lanes()
    return lane & -2, lane >> 5


def pack_first_kernel(t, u, out):
    parts = lane_parts()

    def at_rows(zt, carry):
        rows = rows_of(zt)
        tangent = flow = jnp.zeros(tile, f32)
        for x in range(4):
            tangent = pack_tile(lambda f: t[f, x, rows], range(15), x, tangent, *parts)
            flow = pack_tile(lambda f: u[f, x, rows], range(6), x, flow, *parts)
        out[0, rows] = tangent
        out[1, rows] = flow
        return carry

    lax.fori_loop(0, 8, at_rows, 0)


class PackedLanes:
    def __init__(self):
        lane = lanes()
        field = (lane & 31) >> 1
        tangent = sum(jnp.where(field >= 3 * k, 1, 0) for k in range(1, 5))
        self.high = (lane & 1) == 0
        self.sign = jnp.where(self.high, f32(-1), f32(1))
        self.tangent = tangent
        self.component = field - 3 * tangent
        self.even = gy_even()

    def from_neighbours(self, inner, outer):
        high = jnp.where(self.even, inner, outer)
        low = jnp.where(self.even, outer, inner)
        return jnp.where(self.high, pltpu.roll(high, 127, axis=1), pltpu.roll(low, 1, axis=1))

    def spread_flow(self, flow, at):
        out = None
        for k in range(5):
            turn = (6 * k - 2 * at) % 128
            moved = pltpu.roll(flow, turn, axis=1) if turn else flow
            out = moved if out is None else jnp.where(self.tangent == k, moved, out)
        return out

    def of_component(self, packed, component):
        out = packed
        for i in range(3):
            if i != component:
                out = jnp.where(self.component == i, pltpu.roll(packed, (2 * (i - component)) % 128, axis=1), out)
        return out

    def column_terms(self, scale, tangent, flow, halo, halo_flow, flow_at):
        flag = jnp.where(self.tangent == 4, f32(scale), f32(0))
        speed = self.of_component(self.spread_flow(flow, flow_at), 1)
        weight = scale * viscosity + (0.5 * scale) * self.sign * speed
        made = (0.5 * scale) * self.sign * self.of_component(tangent, 1) + flag
        return weight * halo + made * self.spread_flow(halo_flow, flow_at)


def edge_part(terms, f, edges):
    return jnp.where(edges, pltpu.roll(terms, (127 - 2 * f) % 128, axis=1), 0.0)


def at_edges():
    lane = lanes()
    return (lane == 0) | (lane == 127)


def fill_padding(padded, count):
    for f in range(count):
        padded[f, 0] = jnp.zeros((80, 128), f32)
        padded[f, 5] = jnp.zeros((80, 128), f32)

        def at_plane(x, carry):
            padded[f, x, 0:8] = jnp.zeros(tile, f32)
            padded[f, x, 72:80] = jnp.zeros(tile, f32)
            return carry

        lax.fori_loop(1, 5, at_plane, 0)


def section(padded, members, scale, base, extra, store):
    lane = lanes()
    not_low = jnp.where(lane == 0, f32(0), f32(1))
    not_high = jnp.where(lane == 127, f32(0), f32(1))
    flow_at = 3 * len(members)

    def at_plane(x, carry):
        for zt in range(8):
            first_row = 8 + 8 * zt
            rows = slice(8 * zt, 8 * zt + 8)

            def stencil(f):
                def load(dx, dz):
                    return padded[f, x + 1 + dx, first_row + dz : first_row + dz + 8]

                centre = load(0, 0)
                up, down = pltpu.roll(centre, 127, axis=1), pltpu.roll(centre, 1, axis=1)
                return centre, load(1, 0), load(-1, 0), up, down, load(0, 1), load(0, -1)

            speed, made, bulk = [], [], []
            for i in range(3):
                flow = list(stencil(flow_at + i))
                flow[3], flow[4] = flow[3] * not_high, flow[4] * not_low
                speed.append(flow[0])
                made.append([(-0.5 * scale) * (flow[1 + 2 * j] - flow[2 + 2 * j]) for j in range(3)])
                if 4 in members:
                    total = flow[1] + flow[2] + flow[3] + flow[4] + flow[5] + flow[6]
                    bulk.append(scale * (total - 6.0 * flow[0]))
            halves = [(0.5 * scale) * u for u in speed]
            ahead = [scale * viscosity - h for h in halves]
            behind = [scale * viscosity + h for h in halves]
            ahead[1], behind[1] = ahead[1] * not_high, behind[1] * not_low
            for n, k in enumerate(members):
                around = [stencil(3 * n + i) for i in range(3)]
                for i in range(3):
                    own = around[i]
                    value = (base - 6.0 * viscosity * scale) * own[0]
                    for j in range(3):
                        value += ahead[j] * own[1 + 2 * j] + behind[j] * own[2 + 2 * j]
                        value += made[i][j] * around[j][0]
                    if k == 4:
                        value += bulk[i]
                    if extra is not None:
                        value += 0.5 * extra[3 * k + i, x, rows]
                    store(3 * n + i, x, rows, value)
        return carry

    lax.fori_loop(0, 4, at_plane, 0)


def first_kernel(t, u, columns, *rest):
    outs, padded = rest[:-1], rest[-1]
    fill_padding(padded, 18)

    def copy_plane(x, carry):
        for f in range(15):
            padded[f, x + 1, 8:72] = t[f, x]
        for i in range(3):
            padded[15 + i, x + 1, 8:72] = u[i, x]
        return carry

    lax.fori_loop(0, 4, copy_plane, 0)
    place = {k: (g, n) for g, members in enumerate(groups) for n, k in enumerate(members)}

    def store(f, x, rows, value):
        g, n = place[f // 3]
        outs[g][3 * n + f % 3, x, rows] = value

    section(padded, range(5), time_step, 1.0, None, store)


def halo_terms(scale, sign, speed, tangent):
    weight = scale * viscosity + (0.5 * scale) * sign * speed
    return weight, [(0.5 * scale) * sign * v + (scale if k == 4 else 0.0) for k, v in tangent]


def first_terms_kernel(columns, inner, outer, terms):
    layout = PackedLanes()
    for zt in range(8):
        rows = slice(8 * zt, 8 * zt + 8)
        halo = [layout.from_neighbours(inner[n, rows], outer[n, rows]) for n in range(2)]
        turned = layout.column_terms(time_step, columns[0, rows], columns[1, rows], halo[0], halo[1], 0)
        for x in range(4):
            terms[x, rows] = pltpu.roll(turned, 128 - 32 * x, axis=1) if x else turned


def first_faces_kernel(g, part, terms, t, u, z_in, x_in, z_flow, x_flow, z_out, x_out):
    members = groups[g]
    flow_at = 3 * len(groups[0])
    edges = at_edges()
    for (plane, sign), got, flow_got, out in zip(sides(), (z_in, x_in), (z_flow, x_flow), (z_out, x_out)):
        for zt in range(8):
            rows = slice(8 * zt, 8 * zt + 8)
            here = terms[plane, rows]
            flow_halo = [flow_got[flow_at + i, rows] for i in range(3)]
            tangent = [(k, t[3 * k, plane, rows]) for k in members]
            weight, made = halo_terms(time_step, sign, u[0, plane, rows], tangent)
            for n, k in enumerate(members):
                for i in range(3):
                    j = 3 * n + i
                    value = part[j, plane, rows] + edge_part(here, 3 * k + i, edges)
                    out[j, rows] = value + weight * got[j, rows] + made[n] * flow_halo[i]


def first_whole_kernel(g, part, terms, z_face, x_face, *refs):
    whole, packed = refs[-2:]
    fields = [3 * k + i for k in groups[g] for i in range(3)]
    edges = at_edges()
    lane_facts = lane_parts()
    (z_plane, _), (x_plane, _) = sides()

    def at_rows(zt, carry):
        rows = rows_of(zt)
        total = jnp.zeros(tile, f32)
        for x in (1, 2):
            values = {}
            for j, f in enumerate(fields):
                values[f] = part[j, x, rows] + edge_part(terms[x, rows], f, edges)
                whole[j, x, rows] = values[f]
            total = pack_tile(lambda f: values[f], fields, x, total, *lane_facts)
        for plane, face in ((z_plane, z_face), (x_plane, x_face)):
            values = {}
            for j, f in enumerate(fields):
                values[f] = face[j, rows]
                whole[j, plane, rows] = values[f]
            total = pack_tile(lambda f: values[f], fields, plane, total, *lane_facts)
        packed[rows] = total + refs[0][rows] if g else total
        return carry

    lax.fori_loop(0, 8, at_rows, 0, unroll=2)


def split_refs(refs, *counts):
    pieces, at = [], 0
    for count in counts:
        pieces.append(refs[at : at + count])
        at += count
    pieces.append(refs[at:])
    return pieces


def second_kernel(g, t, u, first, out, padded):
    members = groups[g]
    count = 3 * len(members)
    fill_padding(padded, count + 3)

    def copy_plane(x, carry):
        for j in range(count):
            padded[j, x + 1, 8:72] = first[j, x]
        for i in range(3):
            padded[count + i, x + 1, 8:72] = u[3 + i, x]
        return carry

    lax.fori_loop(0, 4, copy_plane, 0)

    def store(j, x, rows, value):
        out[j, x, rows] = value

    section(padded, members, 0.5 * time_step, 0.5, t, store)


pairs = [(a, b) for a in range(5) for b in range(a, 5)]


def add_products(sums, rows_now, weighted):
    products = [sums[n] + rows_now[a] * rows_now[b] for n, (a, b) in enumerate(pairs)]
    return products + [sums[15 + k] + weighted[k] for k in range(5)]


def second_terms_kernel(packed, columns, inner_flow, outer_flow, inner, outer, terms):
    layout = PackedLanes()
    for zt in range(8):
        rows = slice(8 * zt, 8 * zt + 8)
        halo = layout.from_neighbours(inner[rows], outer[rows])
        halo_flow = layout.from_neighbours(inner_flow[1, rows], outer_flow[1, rows])
        turned = layout.column_terms(0.5 * time_step, packed[rows], columns[1, rows], halo, halo_flow, 3)
        for x in range(4):
            terms[x, rows] = pltpu.roll(turned, 128 - 32 * x, axis=1) if x else turned


def places():
    return {k: (g, 3 * n) for g, members in enumerate(groups) for n, k in enumerate(members)}


def second_inside_kernel(terms, weight, *refs):
    parts, first, (out, sums_out) = split_refs(refs, len(groups), len(groups))
    edges = at_edges()
    place = places()
    sums = [jnp.zeros(tile, f32)] * 20
    for x in (1, 2):

        def at_rows(zt, sums):
            rows = rows_of(zt)
            here = terms[x, rows]
            for i in range(3):
                now, weighted = [], []
                scaled = weight[i, x, rows]
                for k in range(5):
                    g, j = place[k][0], place[k][1] + i
                    value = parts[g][j, x, rows] + edge_part(here, 3 * k + i, edges)
                    out[3 * k + i, x - 1, rows] = value
                    now.append(value)
                    weighted.append(scaled * (first[g][j, x, rows] + value))
                sums = add_products(sums, now, weighted)
            return sums

        sums = lax.fori_loop(0, 8, at_rows, sums, unroll=4)
    for n in range(20):
        sums_out[n] = sums[n]


def second_outer_kernel(u, weight, terms, sums_in, z_flow, x_flow, *refs):
    count = len(groups)
    parts, first, z_in, x_in, (z_out, x_out, sums_out) = split_refs(refs, count, count, count, count)
    last = len(groups) - 1
    flow_at = 3 * len(groups[last]) + (3 if last == 0 else 0)
    scale = 0.5 * time_step
    edges = at_edges()
    place = places()
    sums = [sums_in[n] for n in range(20)]
    for (plane, sign), got, flow_got, out in zip(sides(), (z_in, x_in), (z_flow, x_flow), (z_out, x_out)):

        def at_rows(zt, sums):
            rows = rows_of(zt)
            here = terms[plane, rows]
            flow_halo = [flow_got[flow_at + i, rows] for i in range(3)]
            tangent = [(k, first[place[k][0]][place[k][1], plane, rows]) for k in range(5)]
            outer_weight, made = halo_terms(scale, sign, u[3, plane, rows], tangent)
            for i in range(3):
                now, weighted = [], []
                scaled = weight[i, plane, rows]
                for k in range(5):
                    g, j = place[k][0], place[k][1] + i
                    value = parts[g][j, plane, rows] + edge_part(here, 3 * k + i, edges)
                    value += outer_weight * got[g][j, rows] + made[k] * flow_halo[i]
                    out[3 * k + i, rows] = value
                    now.append(value)
                    weighted.append(scaled * (first[g][j, plane, rows] + value))
                sums = add_products(sums, now, weighted)
            return sums

        sums = lax.fori_loop(0, 8, at_rows, sums, unroll=4)
    stacked = jnp.concatenate([jnp.sum(s, axis=0, keepdims=True) for s in sums] + [jnp.zeros((4, 128), f32)], 0)
    totals = jnp.broadcast_to(jnp.sum(stacked, axis=1, keepdims=True), (24, 128))
    diagonal = lax.broadcasted_iota(jnp.int32, (24, 128), 0) == lax.broadcasted_iota(jnp.int32, (24, 128), 1)
    line = jnp.sum(jnp.where(diagonal, totals, 0.0), axis=0, keepdims=True)
    sums_out[...] = jnp.broadcast_to(line[None], sums_out.shape)


def renorm_kernel(total_cells, inside, z_face, x_face, gathered, out, r_out, c_out, o_out):
    line = jnp.sum(gathered[...], axis=0)
    spread = [jnp.broadcast_to(line[:, n : n + 1], tile) for n in range(20)]
    gram = {pair: spread[n] * f32(1.0 / (3.0 * total_cells)) for n, pair in enumerate(pairs)}
    lower = {}
    for c in range(4):
        value = gram[(c, c)]
        for m in range(c):
            value = value - lower[(c, m)] * lower[(c, m)]
        lower[(c, c)] = jnp.sqrt(value)
        for r in range(c + 1, 4):
            value = gram[(c, r)]
            for m in range(c):
                value = value - lower[(r, m)] * lower[(c, m)]
            lower[(r, c)] = value / lower[(c, c)]
    inverse = {}
    for r in range(4):
        for c in range(r + 1):
            value = jnp.ones(tile, f32) if r == c else jnp.zeros(tile, f32)
            for m in range(c, r):
                value = value - lower[(r, m)] * inverse[(m, c)]
            inverse[(r, c)] = value / lower[(r, r)]
    coefficient = []
    for r in range(4):
        value = inverse[(r, 0)] * gram[(0, 4)]
        for c in range(1, r + 1):
            value = value + inverse[(r, c)] * gram[(c, 4)]
        coefficient.append(value)

    row, lane = lax.broadcasted_iota(jnp.int32, tile, 0), lanes()
    factor, coefficients, objective = (jnp.zeros(tile, f32) for _ in range(3))
    for r in range(4):
        for c in range(r + 1):
            factor = jnp.where((row == c) & (lane == r), lower[(r, c)], factor)
        coefficients = jnp.where(lane == r, coefficient[r], coefficients)
    for k in range(5):
        objective = jnp.where(lane == k, spread[15 + k] * f32(0.5 / total_cells), objective)
    r_out[...] = factor[:4, :4]
    c_out[...] = coefficients[0, :4]
    o_out[...] = objective[0, :5]

    (z_plane, _), (x_plane, _) = sides()
    for plane, load in (
        (1, lambda f, rows: inside[f, 0, rows]),
        (2, lambda f, rows: inside[f, 1, rows]),
        (z_plane, lambda f, rows: z_face[f, rows]),
        (x_plane, lambda f, rows: x_face[f, rows]),
    ):

        def at_rows(zt, carry):
            rows = rows_of(zt)
            for i in range(3):
                now = [load(3 * k + i, rows) for k in range(5)]
                last = now[4]
                for r in range(4):
                    value = inverse[(r, 0)] * now[0]
                    for c in range(1, r + 1):
                        value = value + inverse[(r, c)] * now[c]
                    out[3 * r + i, plane, rows] = value
                    last = last - coefficient[r] * value
                out[12 + i, plane, rows] = last
            return carry

        lax.fori_loop(0, 8, at_rows, 0)


def per_device(tangents, base_flow, objective_weight):
    count_x, count_y = lax.axis_size("gx"), lax.axis_size("gy")
    total_cells = 4 * 64 * 128 * count_x * count_y
    t = tangents.reshape(15, 4, 64, 128)
    u = base_flow.reshape(6, 4, 64, 128)
    last = len(groups) - 1

    def partner(values, axis, count):
        return lax.ppermute(values, axis, [(i, i ^ 1) for i in range(count)])

    def beyond(values, axis, count):
        return lax.ppermute(values, axis, [(i, (i + 2 * (i % 2) - 1) % count) for i in range(count)])

    def after(values, other):
        return lax.optimization_barrier((values, other))[0]

    sizes = [3 * len(members) for members in groups]
    sent = [s + (3 if g == 0 else 0) + (3 if g == last else 0) for g, s in enumerate(sizes)]
    faces = pl.pallas_call(
        faces_kernel,
        out_shape=tuple(shaped(s, 64, 128) for s in sent for _ in range(2)),
        in_specs=[pl.BlockSpec(memory_space=pltpu.HBM)] * 2,
        out_specs=(vmem,) * (2 * len(groups)),
        scratch_shapes=[pltpu.SemaphoreType.DMA((2 * len(groups) + 4,))],
        compiler_params=pltpu.CompilerParams(vmem_limit_bytes=8 << 20),
    )(t, u)
    z_in = [partner(faces[0], "gx", count_x)]
    x_in = [beyond(faces[1], "gx", count_x)]
    columns = call(pack_first_kernel, shaped(2, 64, 128), (t, u))
    inner_in = partner(columns, "gy", count_y)
    outer_in = beyond(after(columns, inner_in), "gy", count_y)
    parts = call(
        first_kernel,
        tuple(shaped(s, 4, 64, 128) for s in sizes),
        (t, u, columns),
        scratch=[pltpu.VMEM((18, 6, 80, 128), f32)],
        flops=10000000,
    )
    for g in range(1, len(groups)):
        z_in.append(partner(after(faces[2 * g], outer_in), "gx", count_x))
        x_in.append(beyond(after(faces[2 * g + 1], outer_in), "gx", count_x))
    terms = call(first_terms_kernel, shaped(4, 64, 128), (columns, inner_in, outer_in))
    first, halves, z_next, x_next = [], [], [], []
    packed = ()
    for g in range(len(groups)):
        if g:
            z_in[g] = after(z_in[g], halves[-1])
        z_face, x_face = call(
            functools.partial(first_faces_kernel, g),
            (shaped(sizes[g], 64, 128), shaped(sizes[g], 64, 128)),
            (parts[g], terms, t, u, z_in[g], x_in[g], z_in[0], x_in[0]),
        )
        z_next.append(partner(z_face, "gx", count_x))
        x_next.append(beyond(x_face, "gx", count_x))
        whole, *packed = call(
            functools.partial(first_whole_kernel, g),
            (shaped(sizes[g], 4, 64, 128), shaped(64, 128)),
            (parts[g], terms, z_face, x_face, *packed),
        )
        first.append(whole)
        halves.append(
            call(
                functools.partial(second_kernel, g),
                shaped(sizes[g], 4, 64, 128),
                (t, u, whole),
                scratch=[pltpu.VMEM((sizes[g] + 3, 6, 80, 128), f32)],
                flops=5000000,
            )
        )
    inner = partner(packed[0], "gy", count_y)
    outer = beyond(after(packed[0], inner), "gy", count_y)
    terms = call(second_terms_kernel, shaped(4, 64, 128), (packed[0], columns, inner_in, outer_in, inner, outer))
    inside, sums = call(
        second_inside_kernel,
        (shaped(15, 2, 64, 128), shaped(20, 8, 128)),
        (terms, objective_weight, *halves, *first),
    )
    z_face, x_face, line = call(
        second_outer_kernel,
        (shaped(15, 64, 128), shaped(15, 64, 128), shaped(count_x * count_y, 1, 128)),
        (u, objective_weight, terms, sums, z_in[last], x_in[last], *halves, *first, *z_next, *x_next),
    )
    gathered = lax.all_to_all(line, ("gx", "gy"), 0, 0, tiled=True)
    renormed, rfactor, coefficients, objective = call(
        functools.partial(renorm_kernel, total_cells),
        (shaped(15, 4, 64, 128), shaped(4, 4), shaped(4), shaped(5)),
        (inside, z_face, x_face, gathered),
    )
    return (renormed.reshape(tangents.shape), rfactor, coefficients, objective)


def solution(mesh):
    placed = (
        P(None, None, "gx", None, "gy"),
        P(None, None, "gx", None, "gy"),
        P(None, "gx", None, "gy"),
    )
    return jax.shard_map(
        per_device,
        mesh=mesh,
        in_specs=placed,
        out_specs=(P(None, None, "gx", None, "gy"), P(), P(), P()),
        check_vma=False,
    )
```

```python
import functools

import jax
import jax.numpy as jnp
from jax import lax
from jax.experimental import pallas as pl
from jax.experimental.pallas import tpu as pltpu
from jax.sharding import PartitionSpec as P

time_step = 0.2
viscosity = 0.05

groups = ((0, 1, 2), (3, 4))

f32 = jnp.float32
vmem = pl.BlockSpec(memory_space=pltpu.VMEM)
tile = (8, 128)


def shaped(*dims):
    return jax.ShapeDtypeStruct(dims, f32)


def call(body, outs, args, scratch=(), flops=1000000, limit=24):
    return pl.pallas_call(
        body,
        out_shape=outs,
        in_specs=[vmem] * len(args),
        out_specs=jax.tree.map(lambda _: vmem, outs),
        scratch_shapes=list(scratch),
        compiler_params=pltpu.CompilerParams(vmem_limit_bytes=limit << 20),
        cost_estimate=pl.CostEstimate(flops=flops, bytes_accessed=4000000, transcendentals=0),
    )(*args)


def lanes():
    return lax.broadcasted_iota(jnp.int32, tile, 1)


def rows_of(zt):
    return pl.ds(pl.multiple_of(zt * 8, 8), 8)


def sides():
    even = lax.rem(lax.axis_index("gx"), 2) == 0
    z_plane = jnp.where(even, 3, 0)
    z_sign = jnp.where(even, f32(-1), f32(1))
    return ((z_plane, z_sign), (3 - z_plane, -z_sign))


def gy_even():
    return lax.rem(lax.axis_index("gy"), 2) == 0


def faces_kernel(chosen, t, u, *refs):
    outs, sem = refs[:-1], refs[-1]
    (z_plane, _), (x_plane, _) = sides()
    last = len(groups) - 1
    copies = []
    for slot, g in enumerate(chosen):
        members = groups[g]
        sources = [(t, 3 * members[0], 3 * len(members))]
        sources += [(u, 0, 3)] if g == 0 else []
        sources += [(u, 3, 3)] if g == last else []
        for side, plane in ((0, z_plane), (1, x_plane)):
            at = 0
            for ref, start, count in sources:
                copies.append(
                    pltpu.make_async_copy(
                        ref.at[pl.ds(start, count), plane],
                        outs[2 * slot + side].at[pl.ds(at, count)],
                        sem.at[len(copies)],
                    )
                )
                at += count
    for copy in copies:
        copy.start()
    for copy in copies:
        copy.wait()


def pack_tile(load, fields, x, packed, even_lane, plane_lane):
    own = jnp.zeros(tile, f32)
    for f in fields:
        own = jnp.where(even_lane == 2 * f, pltpu.roll(load(f), 2 * f + 1, axis=1), own)
    return jnp.where(plane_lane == x, pltpu.roll(own, 32 * x, axis=1), packed)


def lane_parts():
    lane = lanes()
    return lane & -2, lane >> 5


def pack_first_kernel(t, u, face, out):
    parts = lane_parts()

    def at_rows(zt, carry):
        rows = rows_of(zt)
        tangent = flow = jnp.zeros(tile, f32)
        for x in range(4):
            tangent = pack_tile(lambda f: t[f, x, rows], range(15), x, tangent, *parts)
            flow = pack_tile(lambda f: u[f, x, rows], range(6), x, flow, *parts)
        out[0, rows] = tangent
        out[1, rows] = flow
        return carry

    lax.fori_loop(0, 8, at_rows, 0)


class PackedLanes:
    def __init__(self):
        lane = lanes()
        field = (lane & 31) >> 1
        tangent = sum(jnp.where(field >= 3 * k, 1, 0) for k in range(1, 5))
        self.high = (lane & 1) == 0
        self.sign = jnp.where(self.high, f32(-1), f32(1))
        self.tangent = tangent
        self.component = field - 3 * tangent
        self.even = gy_even()

    def from_neighbours(self, inner, outer):
        high = jnp.where(self.even, inner, outer)
        low = jnp.where(self.even, outer, inner)
        return jnp.where(self.high, pltpu.roll(high, 127, axis=1), pltpu.roll(low, 1, axis=1))

    def spread_flow(self, flow, at):
        out = None
        for k in range(5):
            turn = (6 * k - 2 * at) % 128
            moved = pltpu.roll(flow, turn, axis=1) if turn else flow
            out = moved if out is None else jnp.where(self.tangent == k, moved, out)
        return out

    def of_component(self, packed, component):
        out = packed
        for i in range(3):
            if i != component:
                out = jnp.where(self.component == i, pltpu.roll(packed, (2 * (i - component)) % 128, axis=1), out)
        return out

    def column_terms(self, scale, tangent, flow, halo, halo_flow, flow_at):
        flag = jnp.where(self.tangent == 4, f32(scale), f32(0))
        speed = self.of_component(self.spread_flow(flow, flow_at), 1)
        weight = scale * viscosity + (0.5 * scale) * self.sign * speed
        made = (0.5 * scale) * self.sign * self.of_component(tangent, 1) + flag
        return weight * halo + made * self.spread_flow(halo_flow, flow_at)


def edge_part(terms, f, edges):
    return jnp.where(edges, pltpu.roll(terms, (127 - 2 * f) % 128, axis=1), 0.0)


def at_edges():
    lane = lanes()
    return (lane == 0) | (lane == 127)


def fill_padding(padded, count):
    for f in range(count):
        padded[f, 0] = jnp.zeros((80, 128), f32)
        padded[f, 5] = jnp.zeros((80, 128), f32)

        def at_plane(x, carry):
            padded[f, x, 0:8] = jnp.zeros(tile, f32)
            padded[f, x, 72:80] = jnp.zeros(tile, f32)
            return carry

        lax.fori_loop(1, 5, at_plane, 0)


def section(padded, members, scale, base, extra, store):
    lane = lanes()
    not_low = jnp.where(lane == 0, f32(0), f32(1))
    not_high = jnp.where(lane == 127, f32(0), f32(1))
    flow_at = 3 * len(members)

    def at_plane(x, carry):
        for zt in range(8):
            first_row = 8 + 8 * zt
            rows = slice(8 * zt, 8 * zt + 8)

            def stencil(f):
                def load(dx, dz):
                    return padded[f, x + 1 + dx, first_row + dz : first_row + dz + 8]

                centre = load(0, 0)
                up, down = pltpu.roll(centre, 127, axis=1), pltpu.roll(centre, 1, axis=1)
                return centre, load(1, 0), load(-1, 0), up, down, load(0, 1), load(0, -1)

            speed, made, bulk = [], [], []
            for i in range(3):
                flow = list(stencil(flow_at + i))
                flow[3], flow[4] = flow[3] * not_high, flow[4] * not_low
                speed.append(flow[0])
                made.append([(-0.5 * scale) * (flow[1 + 2 * j] - flow[2 + 2 * j]) for j in range(3)])
                if 4 in members:
                    total = flow[1] + flow[2] + flow[3] + flow[4] + flow[5] + flow[6]
                    bulk.append(scale * (total - 6.0 * flow[0]))
            halves = [(0.5 * scale) * u for u in speed]
            ahead = [scale * viscosity - h for h in halves]
            behind = [scale * viscosity + h for h in halves]
            ahead[1], behind[1] = ahead[1] * not_high, behind[1] * not_low
            for n, k in enumerate(members):
                around = [stencil(3 * n + i) for i in range(3)]
                for i in range(3):
                    own = around[i]
                    value = (base - 6.0 * viscosity * scale) * own[0]
                    for j in range(3):
                        value += ahead[j] * own[1 + 2 * j] + behind[j] * own[2 + 2 * j]
                        value += made[i][j] * around[j][0]
                    if k == 4:
                        value += bulk[i]
                    if extra is not None:
                        value += 0.5 * extra[3 * k + i, x, rows]
                    store(3 * n + i, x, rows, value)
        return carry

    lax.fori_loop(0, 4, at_plane, 0)


def first_kernel(t, u, columns, *rest):
    outs, padded = rest[:-1], rest[-1]
    fill_padding(padded, 18)

    def copy_plane(x, carry):
        for f in range(15):
            padded[f, x + 1, 8:72] = t[f, x]
        for i in range(3):
            padded[15 + i, x + 1, 8:72] = u[i, x]
        return carry

    lax.fori_loop(0, 4, copy_plane, 0)
    place = {k: (g, n) for g, members in enumerate(groups) for n, k in enumerate(members)}

    def store(f, x, rows, value):
        g, n = place[f // 3]
        outs[g][3 * n + f % 3, x, rows] = value

    section(padded, range(5), time_step, 1.0, None, store)


def halo_terms(scale, sign, speed, tangent):
    weight = scale * viscosity + (0.5 * scale) * sign * speed
    return weight, [(0.5 * scale) * sign * v + (scale if k == 4 else 0.0) for k, v in tangent]


def first_terms_kernel(columns, inner, outer, terms):
    layout = PackedLanes()
    for zt in range(8):
        rows = slice(8 * zt, 8 * zt + 8)
        halo = [layout.from_neighbours(inner[n, rows], outer[n, rows]) for n in range(2)]
        turned = layout.column_terms(time_step, columns[0, rows], columns[1, rows], halo[0], halo[1], 0)
        for x in range(4):
            terms[x, rows] = pltpu.roll(turned, 128 - 32 * x, axis=1) if x else turned


def first_faces_kernel(g, part, terms, t, u, z_in, x_in, z_flow, x_flow, z_out, x_out):
    members = groups[g]
    flow_at = 3 * len(groups[0])
    edges = at_edges()
    for (plane, sign), got, flow_got, out in zip(sides(), (z_in, x_in), (z_flow, x_flow), (z_out, x_out)):
        for zt in range(8):
            rows = slice(8 * zt, 8 * zt + 8)
            here = terms[plane, rows]
            flow_halo = [flow_got[flow_at + i, rows] for i in range(3)]
            tangent = [(k, t[3 * k, plane, rows]) for k in members]
            weight, made = halo_terms(time_step, sign, u[0, plane, rows], tangent)
            for n, k in enumerate(members):
                for i in range(3):
                    j = 3 * n + i
                    value = part[j, plane, rows] + edge_part(here, 3 * k + i, edges)
                    out[j, rows] = value + weight * got[j, rows] + made[n] * flow_halo[i]


def first_whole_kernel(g, part, terms, z_face, x_face, *refs):
    whole, packed = refs[-2:]
    fields = [3 * k + i for k in groups[g] for i in range(3)]
    edges = at_edges()
    lane_facts = lane_parts()
    (z_plane, _), (x_plane, _) = sides()

    def at_rows(zt, carry):
        rows = rows_of(zt)
        total = jnp.zeros(tile, f32)
        for x in (1, 2):
            values = {}
            for j, f in enumerate(fields):
                values[f] = part[j, x, rows] + edge_part(terms[x, rows], f, edges)
                whole[j, x, rows] = values[f]
            total = pack_tile(lambda f: values[f], fields, x, total, *lane_facts)
        for plane, face in ((z_plane, z_face), (x_plane, x_face)):
            values = {}
            for j, f in enumerate(fields):
                values[f] = face[j, rows]
                whole[j, plane, rows] = values[f]
            total = pack_tile(lambda f: values[f], fields, plane, total, *lane_facts)
        packed[rows] = total + refs[0][rows] if g else total
        return carry

    lax.fori_loop(0, 8, at_rows, 0, unroll=2)


def split_refs(refs, *counts):
    pieces, at = [], 0
    for count in counts:
        pieces.append(refs[at : at + count])
        at += count
    pieces.append(refs[at:])
    return pieces


def second_kernel(g, t, u, first, out, padded):
    members = groups[g]
    count = 3 * len(members)
    fill_padding(padded, count + 3)

    def copy_plane(x, carry):
        for j in range(count):
            padded[j, x + 1, 8:72] = first[j, x]
        for i in range(3):
            padded[count + i, x + 1, 8:72] = u[3 + i, x]
        return carry

    lax.fori_loop(0, 4, copy_plane, 0)

    def store(j, x, rows, value):
        out[j, x, rows] = value

    section(padded, members, 0.5 * time_step, 0.5, t, store)


pairs = [(a, b) for a in range(5) for b in range(a, 5)]


def add_products(sums, rows_now, weighted):
    products = [sums[n] + rows_now[a] * rows_now[b] for n, (a, b) in enumerate(pairs)]
    return products + [sums[15 + k] + weighted[k] for k in range(5)]


def second_terms_kernel(packed, columns, inner_flow, outer_flow, inner, outer, terms):
    layout = PackedLanes()
    for zt in range(8):
        rows = slice(8 * zt, 8 * zt + 8)
        halo = layout.from_neighbours(inner[rows], outer[rows])
        halo_flow = layout.from_neighbours(inner_flow[1, rows], outer_flow[1, rows])
        turned = layout.column_terms(0.5 * time_step, packed[rows], columns[1, rows], halo, halo_flow, 3)
        for x in range(4):
            terms[x, rows] = pltpu.roll(turned, 128 - 32 * x, axis=1) if x else turned


def places():
    return {k: (g, 3 * n) for g, members in enumerate(groups) for n, k in enumerate(members)}


def second_inside_kernel(terms, weight, *refs):
    parts, first, (out, sums_out) = split_refs(refs, len(groups), len(groups))
    edges = at_edges()
    place = places()
    sums = [jnp.zeros(tile, f32)] * 20
    for x in (1, 2):

        def at_rows(zt, sums):
            rows = rows_of(zt)
            here = terms[x, rows]
            for i in range(3):
                now, weighted = [], []
                scaled = weight[i, x, rows]
                for k in range(5):
                    g, j = place[k][0], place[k][1] + i
                    value = parts[g][j, x, rows] + edge_part(here, 3 * k + i, edges)
                    out[3 * k + i, x - 1, rows] = value
                    now.append(value)
                    weighted.append(scaled * (first[g][j, x, rows] + value))
                sums = add_products(sums, now, weighted)
            return sums

        sums = lax.fori_loop(0, 8, at_rows, sums, unroll=4)
    for n in range(20):
        sums_out[n] = sums[n]


def second_outer_kernel(u, weight, terms, sums_in, z_flow, x_flow, *refs):
    count = len(groups)
    parts, first, z_in, x_in, (z_out, x_out, sums_out) = split_refs(refs, count, count, count, count)
    last = len(groups) - 1
    flow_at = 3 * len(groups[last]) + (3 if last == 0 else 0)
    scale = 0.5 * time_step
    edges = at_edges()
    place = places()
    sums = [sums_in[n] for n in range(20)]
    for (plane, sign), got, flow_got, out in zip(sides(), (z_in, x_in), (z_flow, x_flow), (z_out, x_out)):

        def at_rows(zt, sums):
            rows = rows_of(zt)
            here = terms[plane, rows]
            flow_halo = [flow_got[flow_at + i, rows] for i in range(3)]
            tangent = [(k, first[place[k][0]][place[k][1], plane, rows]) for k in range(5)]
            outer_weight, made = halo_terms(scale, sign, u[3, plane, rows], tangent)
            for i in range(3):
                now, weighted = [], []
                scaled = weight[i, plane, rows]
                for k in range(5):
                    g, j = place[k][0], place[k][1] + i
                    value = parts[g][j, plane, rows] + edge_part(here, 3 * k + i, edges)
                    value += outer_weight * got[g][j, rows] + made[k] * flow_halo[i]
                    out[3 * k + i, rows] = value
                    now.append(value)
                    weighted.append(scaled * (first[g][j, plane, rows] + value))
                sums = add_products(sums, now, weighted)
            return sums

        sums = lax.fori_loop(0, 8, at_rows, sums, unroll=4)
    stacked = jnp.concatenate([jnp.sum(s, axis=0, keepdims=True) for s in sums] + [jnp.zeros((4, 128), f32)], 0)
    totals = jnp.broadcast_to(jnp.sum(stacked, axis=1, keepdims=True), (24, 128))
    diagonal = lax.broadcasted_iota(jnp.int32, (24, 128), 0) == lax.broadcasted_iota(jnp.int32, (24, 128), 1)
    line = jnp.sum(jnp.where(diagonal, totals, 0.0), axis=0, keepdims=True)
    sums_out[...] = jnp.broadcast_to(line[None], sums_out.shape)


def renorm_kernel(total_cells, inside, z_face, x_face, gathered, out, r_out, c_out, o_out, ready, sem):
    chains = []
    for first in range(8):
        chain = gathered[first]
        for device in range(first + 8, gathered.shape[0], 8):
            chain = chain + gathered[device]
        chains.append(chain)
    while len(chains) > 1:
        chains = [chains[n] + chains[n + 1] for n in range(0, len(chains), 2)]
    line = chains[0]
    spread = [jnp.broadcast_to(line[:, n : n + 1], tile) for n in range(20)]
    gram = {pair: spread[n] * f32(1.0 / (3.0 * total_cells)) for n, pair in enumerate(pairs)}
    lower, below = {}, {}
    for c in range(4):
        value = gram[(c, c)]
        for m in range(c):
            value = value - lower[(c, m)] * lower[(c, m)]
        lower[(c, c)] = jnp.sqrt(value)
        below[c] = 1.0 / lower[(c, c)]
        for r in range(c + 1, 4):
            value = gram[(c, r)]
            for m in range(c):
                value = value - lower[(r, m)] * lower[(c, m)]
            lower[(r, c)] = value * below[c]
    inverse = {}
    for r in range(4):
        for c in range(r + 1):
            value = jnp.ones(tile, f32) if r == c else jnp.zeros(tile, f32)
            for m in range(c, r):
                value = value - lower[(r, m)] * inverse[(m, c)]
            inverse[(r, c)] = value * below[r]
    coefficient = []
    for r in range(4):
        value = inverse[(r, 0)] * gram[(0, 4)]
        for c in range(1, r + 1):
            value = value + inverse[(r, c)] * gram[(c, 4)]
        coefficient.append(value)

    row, lane = lax.broadcasted_iota(jnp.int32, tile, 0), lanes()
    factor, coefficients, objective = (jnp.zeros(tile, f32) for _ in range(3))
    for r in range(4):
        for c in range(r + 1):
            factor = jnp.where((row == c) & (lane == r), lower[(r, c)], factor)
        coefficients = jnp.where(lane == r, coefficient[r], coefficients)
    for k in range(5):
        objective = jnp.where(lane == k, spread[15 + k] * f32(0.5 / total_cells), objective)
    r_out[...] = factor[:4, :4]
    c_out[...] = coefficients[0, :4]
    o_out[...] = objective[0, :5]

    (z_plane, _), (x_plane, _) = sides()
    copies = []
    for plane, load in (
        (1, lambda f, rows: inside[f, 0, rows]),
        (2, lambda f, rows: inside[f, 1, rows]),
        (z_plane, lambda f, rows: z_face[f, rows]),
        (x_plane, lambda f, rows: x_face[f, rows]),
    ):

        def at_rows(zt, carry):
            rows = rows_of(zt)
            for i in range(3):
                now = [load(3 * k + i, rows) for k in range(5)]
                last = now[4]
                for r in range(4):
                    value = inverse[(r, 0)] * now[0]
                    for c in range(1, r + 1):
                        value = value + inverse[(r, c)] * now[c]
                    ready[3 * r + i, plane, rows] = value
                    last = last - coefficient[r] * value
                ready[12 + i, plane, rows] = last
            return carry

        lax.fori_loop(0, 8, at_rows, 0, unroll=4)
        copy = pltpu.make_async_copy(ready.at[:, plane], out.at[:, plane], sem.at[len(copies)])
        copy.start()
        copies.append(copy)
    for copy in copies:
        copy.wait()


def per_device(tangents, base_flow, objective_weight):
    count_x, count_y = lax.axis_size("gx"), lax.axis_size("gy")
    total_cells = 4 * 64 * 128 * count_x * count_y
    t = tangents.reshape(15, 4, 64, 128)
    u = base_flow.reshape(6, 4, 64, 128)
    last = len(groups) - 1

    def partner(values, axis, count):
        return lax.ppermute(values, axis, [(i, i ^ 1) for i in range(count)])

    def beyond(values, axis, count):
        return lax.ppermute(values, axis, [(i, (i + 2 * (i % 2) - 1) % count) for i in range(count)])

    def after(values, other):
        return lax.optimization_barrier((values, other))[0]

    sizes = [3 * len(members) for members in groups]
    sent = [s + (3 if g == 0 else 0) + (3 if g == last else 0) for g, s in enumerate(sizes)]
    def send_buffers(chosen, limit):
        return pl.pallas_call(
            functools.partial(faces_kernel, chosen),
            out_shape=tuple(shaped(sent[g], 64, 128) for g in chosen for _ in range(2)),
            in_specs=[pl.BlockSpec(memory_space=pltpu.HBM)] * 2,
            out_specs=(vmem,) * (2 * len(chosen)),
            scratch_shapes=[pltpu.SemaphoreType.DMA((2 * len(chosen) + 4,))],
            compiler_params=pltpu.CompilerParams(vmem_limit_bytes=limit),
        )(t, u)

    faces = [*send_buffers((0,), None), *send_buffers(tuple(range(1, len(groups))), 8 << 20)]
    z_in = [partner(faces[0], "gx", count_x)]
    x_in = [beyond(faces[1], "gx", count_x)]
    columns = call(pack_first_kernel, shaped(2, 64, 128), (t, u, faces[1]))
    inner_in = partner(columns, "gy", count_y)
    outer_in = beyond(after(columns, inner_in), "gy", count_y)
    parts = call(
        first_kernel,
        tuple(shaped(s, 4, 64, 128) for s in sizes),
        (t, u, columns),
        scratch=[pltpu.VMEM((18, 6, 80, 128), f32)],
        flops=10000000,
    )
    for g in range(1, len(groups)):
        z_in.append(partner(after(faces[2 * g], outer_in), "gx", count_x))
        x_in.append(beyond(after(faces[2 * g + 1], outer_in), "gx", count_x))
    terms = call(first_terms_kernel, shaped(4, 64, 128), (columns, inner_in, outer_in))
    first, halves, z_next, x_next = [], [], [], []
    packed = ()
    for g in range(len(groups)):
        if g:
            z_in[g] = after(z_in[g], halves[-1])
        z_face, x_face = call(
            functools.partial(first_faces_kernel, g),
            (shaped(sizes[g], 64, 128), shaped(sizes[g], 64, 128)),
            (parts[g], terms, t, u, z_in[g], x_in[g], z_in[0], x_in[0]),
        )
        z_next.append(partner(z_face, "gx", count_x))
        x_next.append(beyond(x_face, "gx", count_x))
        whole, *packed = call(
            functools.partial(first_whole_kernel, g),
            (shaped(sizes[g], 4, 64, 128), shaped(64, 128)),
            (parts[g], terms, z_face, x_face, *packed),
        )
        first.append(whole)
        halves.append(
            call(
                functools.partial(second_kernel, g),
                shaped(sizes[g], 4, 64, 128),
                (t, u, whole),
                scratch=[pltpu.VMEM((sizes[g] + 3, 6, 80, 128), f32)],
                flops=5000000,
            )
        )
    inner = partner(packed[0], "gy", count_y)
    outer = beyond(after(packed[0], inner), "gy", count_y)
    terms = call(second_terms_kernel, shaped(4, 64, 128), (packed[0], columns, inner_in, outer_in, inner, outer))
    inside, sums = call(
        second_inside_kernel,
        (shaped(15, 2, 64, 128), shaped(20, 8, 128)),
        (terms, objective_weight, *halves, *first),
    )
    z_face, x_face, line = call(
        second_outer_kernel,
        (shaped(15, 64, 128), shaped(15, 64, 128), shaped(count_x * count_y, 1, 128)),
        (u, objective_weight, terms, sums, z_in[last], x_in[last], *halves, *first, *z_next, *x_next),
    )
    gathered = lax.all_to_all(line, ("gx", "gy"), 0, 0, tiled=True)
    renormed, rfactor, coefficients, objective = pl.pallas_call(
        functools.partial(renorm_kernel, total_cells),
        out_shape=(shaped(15, 4, 64, 128), shaped(4, 4), shaped(4), shaped(5)),
        in_specs=[vmem] * 4,
        out_specs=(pl.BlockSpec(memory_space=pl.ANY), vmem, vmem, vmem),
        scratch_shapes=[pltpu.VMEM((15, 4, 64, 128), f32), pltpu.SemaphoreType.DMA((4,))],
        compiler_params=pltpu.CompilerParams(vmem_limit_bytes=24 << 20),
    )(inside, z_face, x_face, gathered)
    return (renormed.reshape(tangents.shape), rfactor, coefficients, objective)


def solution(mesh):
    placed = (
        P(None, None, "gx", None, "gy"),
        P(None, None, "gx", None, "gy"),
        P(None, "gx", None, "gy"),
    )
    return jax.shard_map(
        per_device,
        mesh=mesh,
        in_specs=placed,
        out_specs=(P(None, None, "gx", None, "gy"), P(), P(), P()),
        check_vma=False,
    )
```

```python
import functools

import jax
import jax.numpy as jnp
from jax import lax
from jax.experimental import pallas as pl
from jax.experimental.pallas import tpu as pltpu
from jax.sharding import PartitionSpec as P

time_step = 0.2
viscosity = 0.05

groups = ((0, 1, 2), (3, 4))

f32 = jnp.float32
vmem = pl.BlockSpec(memory_space=pltpu.VMEM)
tile = (8, 128)


def shaped(*dims):
    return jax.ShapeDtypeStruct(dims, f32)


def call(body, outs, args, scratch=(), flops=1000000, limit=24):
    return pl.pallas_call(
        body,
        out_shape=outs,
        in_specs=[vmem] * len(args),
        out_specs=jax.tree.map(lambda _: vmem, outs),
        scratch_shapes=list(scratch),
        compiler_params=pltpu.CompilerParams(vmem_limit_bytes=limit << 20),
        cost_estimate=pl.CostEstimate(flops=flops, bytes_accessed=4000000, transcendentals=0),
    )(*args)


def lanes():
    return lax.broadcasted_iota(jnp.int32, tile, 1)


def rows_of(zt):
    return pl.ds(pl.multiple_of(zt * 8, 8), 8)


def sides():
    even = lax.rem(lax.axis_index("gx"), 2) == 0
    z_plane = jnp.where(even, 3, 0)
    z_sign = jnp.where(even, f32(-1), f32(1))
    return ((z_plane, z_sign), (3 - z_plane, -z_sign))


def gy_even():
    return lax.rem(lax.axis_index("gy"), 2) == 0


def faces_kernel(chosen, t, u, *refs):
    outs, sem = refs[:-1], refs[-1]
    (z_plane, _), (x_plane, _) = sides()
    copies = []
    for slot, g in enumerate(chosen):
        members = groups[g]
        sources = [(t, 3 * members[0], 3 * len(members))]
        sources += [(u, 0, 3)] if g == 0 else []
        for side, plane in ((0, z_plane), (1, x_plane)):
            at = 0
            for ref, start, count in sources:
                copies.append(
                    pltpu.make_async_copy(
                        ref.at[pl.ds(start, count), plane],
                        outs[2 * slot + side].at[pl.ds(at, count)],
                        sem.at[len(copies)],
                    )
                )
                at += count
    for copy in copies:
        copy.start()
    for copy in copies:
        copy.wait()


def pack_tile(load, fields, x, packed, even_lane, plane_lane):
    own = jnp.zeros(tile, f32)
    for f in fields:
        own = jnp.where(even_lane == 2 * f, pltpu.roll(load(f), 2 * f + 1, axis=1), own)
    return jnp.where(plane_lane == x, pltpu.roll(own, 32 * x, axis=1), packed)


def lane_parts():
    lane = lanes()
    return lane & -2, lane >> 5


def pack_first_kernel(t, u, face, out):
    parts = lane_parts()

    def at_rows(zt, carry):
        rows = rows_of(zt)
        tangent = flow = jnp.zeros(tile, f32)
        for x in range(4):
            tangent = pack_tile(lambda f: t[f, x, rows], range(15), x, tangent, *parts)
            flow = pack_tile(lambda f: u[f, x, rows], range(6), x, flow, *parts)
        out[0, rows] = tangent
        out[1, rows] = flow
        return carry

    lax.fori_loop(0, 8, at_rows, 0)


class PackedLanes:
    def __init__(self):
        lane = lanes()
        field = (lane & 31) >> 1
        tangent = sum(jnp.where(field >= 3 * k, 1, 0) for k in range(1, 5))
        self.high = (lane & 1) == 0
        self.sign = jnp.where(self.high, f32(-1), f32(1))
        self.tangent = tangent
        self.component = field - 3 * tangent
        self.even = gy_even()

    def from_neighbours(self, inner, outer):
        high = jnp.where(self.even, inner, outer)
        low = jnp.where(self.even, outer, inner)
        return jnp.where(self.high, pltpu.roll(high, 127, axis=1), pltpu.roll(low, 1, axis=1))

    def spread_flow(self, flow, at):
        out = None
        for k in range(5):
            turn = (6 * k - 2 * at) % 128
            moved = pltpu.roll(flow, turn, axis=1) if turn else flow
            out = moved if out is None else jnp.where(self.tangent == k, moved, out)
        return out

    def of_component(self, packed, component):
        out = packed
        for i in range(3):
            if i != component:
                out = jnp.where(self.component == i, pltpu.roll(packed, (2 * (i - component)) % 128, axis=1), out)
        return out

    def column_terms(self, scale, tangent, flow, halo, halo_flow, flow_at):
        flag = jnp.where(self.tangent == 4, f32(scale), f32(0))
        speed = self.of_component(self.spread_flow(flow, flow_at), 1)
        weight = scale * viscosity + (0.5 * scale) * self.sign * speed
        made = (0.5 * scale) * self.sign * self.of_component(tangent, 1) + flag
        return weight * halo + made * self.spread_flow(halo_flow, flow_at)


def edge_part(terms, f, edges):
    return jnp.where(edges, pltpu.roll(terms, (127 - 2 * f) % 128, axis=1), 0.0)


def at_edges():
    lane = lanes()
    return (lane == 0) | (lane == 127)


def fill_padding(padded, count):
    for f in range(count):
        padded[f, 0] = jnp.zeros((80, 128), f32)
        padded[f, 5] = jnp.zeros((80, 128), f32)

        def at_plane(x, carry):
            padded[f, x, 0:8] = jnp.zeros(tile, f32)
            padded[f, x, 72:80] = jnp.zeros(tile, f32)
            return carry

        lax.fori_loop(1, 5, at_plane, 0)


def section(padded, members, scale, base, extra, store):
    lane = lanes()
    not_low = jnp.where(lane == 0, f32(0), f32(1))
    not_high = jnp.where(lane == 127, f32(0), f32(1))
    flow_at = 3 * len(members)

    def at_plane(x, carry):
        for zt in range(8):
            first_row = 8 + 8 * zt
            rows = slice(8 * zt, 8 * zt + 8)

            def stencil(f):
                def load(dx, dz):
                    return padded[f, x + 1 + dx, first_row + dz : first_row + dz + 8]

                centre = load(0, 0)
                up, down = pltpu.roll(centre, 127, axis=1), pltpu.roll(centre, 1, axis=1)
                return centre, load(1, 0), load(-1, 0), up, down, load(0, 1), load(0, -1)

            speed, made, bulk = [], [], []
            for i in range(3):
                flow = list(stencil(flow_at + i))
                flow[3], flow[4] = flow[3] * not_high, flow[4] * not_low
                speed.append(flow[0])
                made.append([(-0.5 * scale) * (flow[1 + 2 * j] - flow[2 + 2 * j]) for j in range(3)])
                if 4 in members:
                    total = flow[1] + flow[2] + flow[3] + flow[4] + flow[5] + flow[6]
                    bulk.append(scale * (total - 6.0 * flow[0]))
            halves = [(0.5 * scale) * u for u in speed]
            ahead = [scale * viscosity - h for h in halves]
            behind = [scale * viscosity + h for h in halves]
            ahead[1], behind[1] = ahead[1] * not_high, behind[1] * not_low
            for n, k in enumerate(members):
                around = [stencil(3 * n + i) for i in range(3)]
                for i in range(3):
                    own = around[i]
                    value = (base - 6.0 * viscosity * scale) * own[0]
                    for j in range(3):
                        value += ahead[j] * own[1 + 2 * j] + behind[j] * own[2 + 2 * j]
                        value += made[i][j] * around[j][0]
                    if k == 4:
                        value += bulk[i]
                    if extra is not None:
                        value += 0.5 * extra[3 * k + i, x, rows]
                    store(3 * n + i, x, rows, value)
        return carry

    lax.fori_loop(0, 4, at_plane, 0)


def first_kernel(t, u, columns, *rest):
    outs, padded = rest[:-1], rest[-1]
    fill_padding(padded, 18)

    def copy_plane(x, carry):
        for f in range(15):
            padded[f, x + 1, 8:72] = t[f, x]
        for i in range(3):
            padded[15 + i, x + 1, 8:72] = u[i, x]
        return carry

    lax.fori_loop(0, 4, copy_plane, 0)
    place = {k: (g, n) for g, members in enumerate(groups) for n, k in enumerate(members)}

    def store(f, x, rows, value):
        g, n = place[f // 3]
        outs[g][3 * n + f % 3, x, rows] = value

    section(padded, range(5), time_step, 1.0, None, store)


def halo_terms(scale, sign, speed, tangent):
    weight = scale * viscosity + (0.5 * scale) * sign * speed
    return weight, [(0.5 * scale) * sign * v + (scale if k == 4 else 0.0) for k, v in tangent]


def first_terms_kernel(columns, inner, outer, terms):
    layout = PackedLanes()
    for zt in range(8):
        rows = slice(8 * zt, 8 * zt + 8)
        halo = [layout.from_neighbours(inner[n, rows], outer[n, rows]) for n in range(2)]
        turned = layout.column_terms(time_step, columns[0, rows], columns[1, rows], halo[0], halo[1], 0)
        for x in range(4):
            terms[x, rows] = pltpu.roll(turned, 128 - 32 * x, axis=1) if x else turned


def first_faces_kernel(g, part, terms, t, u, z_in, x_in, z_flow, x_flow, z_out, x_out):
    members = groups[g]
    flow_at = 3 * len(groups[0])
    edges = at_edges()
    for (plane, sign), got, flow_got, out in zip(sides(), (z_in, x_in), (z_flow, x_flow), (z_out, x_out)):
        if g == 0:
            for i in range(3):
                out[flow_at + i] = u[3 + i, plane]
        for zt in range(8):
            rows = slice(8 * zt, 8 * zt + 8)
            here = terms[plane, rows]
            flow_halo = [flow_got[flow_at + i, rows] for i in range(3)]
            tangent = [(k, t[3 * k, plane, rows]) for k in members]
            weight, made = halo_terms(time_step, sign, u[0, plane, rows], tangent)
            for n, k in enumerate(members):
                for i in range(3):
                    j = 3 * n + i
                    value = part[j, plane, rows] + edge_part(here, 3 * k + i, edges)
                    out[j, rows] = value + weight * got[j, rows] + made[n] * flow_halo[i]


def first_whole_kernel(g, part, terms, z_face, x_face, *refs):
    whole, packed = refs[-2:]
    fields = [3 * k + i for k in groups[g] for i in range(3)]
    edges = at_edges()
    lane_facts = lane_parts()
    (z_plane, _), (x_plane, _) = sides()

    def at_rows(zt, carry):
        rows = rows_of(zt)
        total = jnp.zeros(tile, f32)
        for x in (1, 2):
            values = {}
            for j, f in enumerate(fields):
                values[f] = part[j, x, rows] + edge_part(terms[x, rows], f, edges)
                whole[j, x, rows] = values[f]
            total = pack_tile(lambda f: values[f], fields, x, total, *lane_facts)
        for plane, face in ((z_plane, z_face), (x_plane, x_face)):
            values = {}
            for j, f in enumerate(fields):
                values[f] = face[j, rows]
                whole[j, plane, rows] = values[f]
            total = pack_tile(lambda f: values[f], fields, plane, total, *lane_facts)
        packed[rows] = total + refs[0][rows] if g else total
        return carry

    lax.fori_loop(0, 8, at_rows, 0, unroll=2)


def split_refs(refs, *counts):
    pieces, at = [], 0
    for count in counts:
        pieces.append(refs[at : at + count])
        at += count
    pieces.append(refs[at:])
    return pieces


def second_kernel(g, t, u, first, out, padded):
    members = groups[g]
    count = 3 * len(members)
    fill_padding(padded, count + 3)

    def copy_plane(x, carry):
        for j in range(count):
            padded[j, x + 1, 8:72] = first[j, x]
        for i in range(3):
            padded[count + i, x + 1, 8:72] = u[3 + i, x]
        return carry

    lax.fori_loop(0, 4, copy_plane, 0)

    def store(j, x, rows, value):
        out[j, x, rows] = value

    section(padded, members, 0.5 * time_step, 0.5, t, store)


pairs = [(a, b) for a in range(5) for b in range(a, 5)]


def add_products(sums, rows_now, weighted):
    products = [sums[n] + rows_now[a] * rows_now[b] for n, (a, b) in enumerate(pairs)]
    return products + [sums[15 + k] + weighted[k] for k in range(5)]


def second_terms_kernel(packed, columns, inner_flow, outer_flow, inner, outer, terms):
    layout = PackedLanes()
    for zt in range(8):
        rows = slice(8 * zt, 8 * zt + 8)
        halo = layout.from_neighbours(inner[rows], outer[rows])
        halo_flow = layout.from_neighbours(inner_flow[1, rows], outer_flow[1, rows])
        turned = layout.column_terms(0.5 * time_step, packed[rows], columns[1, rows], halo, halo_flow, 3)
        for x in range(4):
            terms[x, rows] = pltpu.roll(turned, 128 - 32 * x, axis=1) if x else turned


def places():
    return {k: (g, 3 * n) for g, members in enumerate(groups) for n, k in enumerate(members)}


def second_inside_kernel(terms, weight, *refs):
    parts, first, (out, sums_out) = split_refs(refs, len(groups), len(groups))
    edges = at_edges()
    place = places()
    sums = [jnp.zeros(tile, f32)] * 20
    for x in (1, 2):

        def at_rows(zt, sums):
            rows = rows_of(zt)
            here = terms[x, rows]
            for i in range(3):
                now, weighted = [], []
                scaled = weight[i, x, rows]
                for k in range(5):
                    g, j = place[k][0], place[k][1] + i
                    value = parts[g][j, x, rows] + edge_part(here, 3 * k + i, edges)
                    out[3 * k + i, x - 1, rows] = value
                    now.append(value)
                    weighted.append(scaled * (first[g][j, x, rows] + value))
                sums = add_products(sums, now, weighted)
            return sums

        sums = lax.fori_loop(0, 8, at_rows, sums, unroll=4)
    for n in range(20):
        sums_out[n] = sums[n]


def second_outer_kernel(u, weight, terms, sums_in, z_flow, x_flow, *refs):
    count = len(groups)
    parts, first, z_in, x_in, (z_out, x_out, sums_out) = split_refs(refs, count, count, count, count)
    flow_at = 3 * len(groups[0])
    scale = 0.5 * time_step
    edges = at_edges()
    place = places()
    sums = [sums_in[n] for n in range(20)]
    for (plane, sign), got, flow_got, out in zip(sides(), (z_in, x_in), (z_flow, x_flow), (z_out, x_out)):

        def at_rows(zt, sums):
            rows = rows_of(zt)
            here = terms[plane, rows]
            flow_halo = [flow_got[flow_at + i, rows] for i in range(3)]
            tangent = [(k, first[place[k][0]][place[k][1], plane, rows]) for k in range(5)]
            outer_weight, made = halo_terms(scale, sign, u[3, plane, rows], tangent)
            for i in range(3):
                now, weighted = [], []
                scaled = weight[i, plane, rows]
                for k in range(5):
                    g, j = place[k][0], place[k][1] + i
                    value = parts[g][j, plane, rows] + edge_part(here, 3 * k + i, edges)
                    value += outer_weight * got[g][j, rows] + made[k] * flow_halo[i]
                    out[3 * k + i, rows] = value
                    now.append(value)
                    weighted.append(scaled * (first[g][j, plane, rows] + value))
                sums = add_products(sums, now, weighted)
            return sums

        sums = lax.fori_loop(0, 8, at_rows, sums, unroll=4)
    stacked = jnp.concatenate([jnp.sum(s, axis=0, keepdims=True) for s in sums] + [jnp.zeros((4, 128), f32)], 0)
    totals = jnp.broadcast_to(jnp.sum(stacked, axis=1, keepdims=True), (24, 128))
    diagonal = lax.broadcasted_iota(jnp.int32, (24, 128), 0) == lax.broadcasted_iota(jnp.int32, (24, 128), 1)
    line = jnp.sum(jnp.where(diagonal, totals, 0.0), axis=0, keepdims=True)
    sums_out[...] = jnp.broadcast_to(line[None], sums_out.shape)


def renorm_kernel(total_cells, inside, z_face, x_face, gathered, out, r_out, c_out, o_out, ready, sem):
    chains = []
    for first in range(8):
        chain = gathered[first]
        for device in range(first + 8, gathered.shape[0], 8):
            chain = chain + gathered[device]
        chains.append(chain)
    while len(chains) > 1:
        chains = [chains[n] + chains[n + 1] for n in range(0, len(chains), 2)]
    line = chains[0]
    spread = [jnp.broadcast_to(line[:, n : n + 1], tile) for n in range(20)]
    gram = {pair: spread[n] * f32(1.0 / (3.0 * total_cells)) for n, pair in enumerate(pairs)}
    lower, below = {}, {}
    for c in range(4):
        value = gram[(c, c)]
        for m in range(c):
            value = value - lower[(c, m)] * lower[(c, m)]
        lower[(c, c)] = jnp.sqrt(value)
        below[c] = 1.0 / lower[(c, c)]
        for r in range(c + 1, 4):
            value = gram[(c, r)]
            for m in range(c):
                value = value - lower[(r, m)] * lower[(c, m)]
            lower[(r, c)] = value * below[c]
    inverse = {}
    for r in range(4):
        for c in range(r + 1):
            value = jnp.ones(tile, f32) if r == c else jnp.zeros(tile, f32)
            for m in range(c, r):
                value = value - lower[(r, m)] * inverse[(m, c)]
            inverse[(r, c)] = value * below[r]
    coefficient = []
    for r in range(4):
        value = inverse[(r, 0)] * gram[(0, 4)]
        for c in range(1, r + 1):
            value = value + inverse[(r, c)] * gram[(c, 4)]
        coefficient.append(value)

    row, lane = lax.broadcasted_iota(jnp.int32, tile, 0), lanes()
    factor, coefficients, objective = (jnp.zeros(tile, f32) for _ in range(3))
    for r in range(4):
        for c in range(r + 1):
            factor = jnp.where((row == c) & (lane == r), lower[(r, c)], factor)
        coefficients = jnp.where(lane == r, coefficient[r], coefficients)
    for k in range(5):
        objective = jnp.where(lane == k, spread[15 + k] * f32(0.5 / total_cells), objective)
    r_out[...] = factor[:4, :4]
    c_out[...] = coefficients[0, :4]
    o_out[...] = objective[0, :5]

    (z_plane, _), (x_plane, _) = sides()
    copies = []
    for plane, load in (
        (1, lambda f, rows: inside[f, 0, rows]),
        (2, lambda f, rows: inside[f, 1, rows]),
        (z_plane, lambda f, rows: z_face[f, rows]),
        (x_plane, lambda f, rows: x_face[f, rows]),
    ):

        def at_rows(zt, carry):
            rows = rows_of(zt)
            for i in range(3):
                now = [load(3 * k + i, rows) for k in range(5)]
                last = now[4]
                for r in range(4):
                    value = inverse[(r, 0)] * now[0]
                    for c in range(1, r + 1):
                        value = value + inverse[(r, c)] * now[c]
                    ready[3 * r + i, plane, rows] = value
                    last = last - coefficient[r] * value
                ready[12 + i, plane, rows] = last
            return carry

        lax.fori_loop(0, 8, at_rows, 0, unroll=4)
        copy = pltpu.make_async_copy(ready.at[:, plane], out.at[:, plane], sem.at[len(copies)])
        copy.start()
        copies.append(copy)
    for copy in copies:
        copy.wait()


def per_device(tangents, base_flow, objective_weight):
    count_x, count_y = lax.axis_size("gx"), lax.axis_size("gy")
    total_cells = 4 * 64 * 128 * count_x * count_y
    t = tangents.reshape(15, 4, 64, 128)
    u = base_flow.reshape(6, 4, 64, 128)
    last = len(groups) - 1

    def partner(values, axis, count):
        return lax.ppermute(values, axis, [(i, i ^ 1) for i in range(count)])

    def beyond(values, axis, count):
        return lax.ppermute(values, axis, [(i, (i + 2 * (i % 2) - 1) % count) for i in range(count)])

    def after(values, other):
        return lax.optimization_barrier((values, other))[0]

    sizes = [3 * len(members) for members in groups]
    sent = [s + (3 if g == 0 else 0) for g, s in enumerate(sizes)]
    def send_buffers(chosen, limit):
        return pl.pallas_call(
            functools.partial(faces_kernel, chosen),
            out_shape=tuple(shaped(sent[g], 64, 128) for g in chosen for _ in range(2)),
            in_specs=[pl.BlockSpec(memory_space=pltpu.HBM)] * 2,
            out_specs=(vmem,) * (2 * len(chosen)),
            scratch_shapes=[pltpu.SemaphoreType.DMA((2 * len(chosen) + 4,))],
            compiler_params=pltpu.CompilerParams(vmem_limit_bytes=limit),
        )(t, u)

    faces = [*send_buffers((0,), None), *send_buffers(tuple(range(1, len(groups))), 8 << 20)]
    z_in = [partner(faces[0], "gx", count_x)]
    x_in = [beyond(faces[1], "gx", count_x)]
    columns = call(pack_first_kernel, shaped(2, 64, 128), (t, u, faces[1]))
    inner_in = partner(columns, "gy", count_y)
    outer_in = beyond(after(columns, inner_in), "gy", count_y)
    parts = call(
        first_kernel,
        tuple(shaped(s, 4, 64, 128) for s in sizes),
        (t, u, columns),
        scratch=[pltpu.VMEM((18, 6, 80, 128), f32)],
        flops=10000000,
    )
    for g in range(1, len(groups)):
        z_in.append(partner(after(faces[2 * g], outer_in), "gx", count_x))
        x_in.append(beyond(after(faces[2 * g + 1], outer_in), "gx", count_x))
    terms = call(first_terms_kernel, shaped(4, 64, 128), (columns, inner_in, outer_in))
    first, halves, z_next, x_next = [], [], [], []
    packed = ()
    for g in range(len(groups)):
        if g:
            z_in[g] = after(z_in[g], halves[-1])
        z_face, x_face = call(
            functools.partial(first_faces_kernel, g),
            (shaped(sent[g], 64, 128), shaped(sent[g], 64, 128)),
            (parts[g], terms, t, u, z_in[g], x_in[g], z_in[0], x_in[0]),
        )
        z_next.append(partner(z_face, "gx", count_x))
        x_next.append(beyond(x_face, "gx", count_x))
        whole, *packed = call(
            functools.partial(first_whole_kernel, g),
            (shaped(sizes[g], 4, 64, 128), shaped(64, 128)),
            (parts[g], terms, z_face, x_face, *packed),
        )
        first.append(whole)
        halves.append(
            call(
                functools.partial(second_kernel, g),
                shaped(sizes[g], 4, 64, 128),
                (t, u, whole),
                scratch=[pltpu.VMEM((sizes[g] + 3, 6, 80, 128), f32)],
                flops=5000000,
            )
        )
    inner = partner(packed[0], "gy", count_y)
    outer = beyond(after(packed[0], inner), "gy", count_y)
    terms = call(second_terms_kernel, shaped(4, 64, 128), (packed[0], columns, inner_in, outer_in, inner, outer))
    inside, sums = call(
        second_inside_kernel,
        (shaped(15, 2, 64, 128), shaped(20, 8, 128)),
        (terms, objective_weight, *halves, *first),
    )
    z_face, x_face, line = call(
        second_outer_kernel,
        (shaped(15, 64, 128), shaped(15, 64, 128), shaped(count_x * count_y, 1, 128)),
        (u, objective_weight, terms, sums, z_next[0], x_next[0], *halves, *first, *z_next, *x_next),
    )
    gathered = lax.all_to_all(line, ("gx", "gy"), 0, 0, tiled=True)
    renormed, rfactor, coefficients, objective = pl.pallas_call(
        functools.partial(renorm_kernel, total_cells),
        out_shape=(shaped(15, 4, 64, 128), shaped(4, 4), shaped(4), shaped(5)),
        in_specs=[vmem] * 4,
        out_specs=(pl.BlockSpec(memory_space=pl.ANY), vmem, vmem, vmem),
        scratch_shapes=[pltpu.VMEM((15, 4, 64, 128), f32), pltpu.SemaphoreType.DMA((4,))],
        compiler_params=pltpu.CompilerParams(vmem_limit_bytes=24 << 20),
    )(inside, z_face, x_face, gathered)
    return (renormed.reshape(tangents.shape), rfactor, coefficients, objective)


def solution(mesh):
    placed = (
        P(None, None, "gx", None, "gy"),
        P(None, None, "gx", None, "gy"),
        P(None, "gx", None, "gy"),
    )
    return jax.shard_map(
        per_device,
        mesh=mesh,
        in_specs=placed,
        out_specs=(P(None, None, "gx", None, "gy"), P(), P(), P()),
        check_vma=False,
    )
```

```python
import functools

import jax
import jax.numpy as jnp
from jax import lax
from jax.experimental import pallas as pl
from jax.experimental.pallas import tpu as pltpu
from jax.sharding import PartitionSpec as P

time_step = 0.2
viscosity = 0.05

groups = ((0, 1, 2), (3, 4))

f32 = jnp.float32
vmem = pl.BlockSpec(memory_space=pltpu.VMEM)
tile = (8, 128)


def shaped(*dims):
    return jax.ShapeDtypeStruct(dims, f32)


def call(body, outs, args, scratch=(), flops=1000000, limit=24):
    return pl.pallas_call(
        body,
        out_shape=outs,
        in_specs=[vmem] * len(args),
        out_specs=jax.tree.map(lambda _: vmem, outs),
        scratch_shapes=list(scratch),
        compiler_params=pltpu.CompilerParams(vmem_limit_bytes=limit << 20),
        cost_estimate=pl.CostEstimate(flops=flops, bytes_accessed=4000000, transcendentals=0),
    )(*args)


def lanes():
    return lax.broadcasted_iota(jnp.int32, tile, 1)


def rows_of(zt):
    return pl.ds(pl.multiple_of(zt * 8, 8), 8)


def sides():
    even = lax.rem(lax.axis_index("gx"), 2) == 0
    z_plane = jnp.where(even, 3, 0)
    z_sign = jnp.where(even, f32(-1), f32(1))
    return ((z_plane, z_sign), (3 - z_plane, -z_sign))


def gy_even():
    return lax.rem(lax.axis_index("gy"), 2) == 0


def faces_kernel(chosen, t, u, *refs):
    outs, sem = refs[:-1], refs[-1]
    (z_plane, _), (x_plane, _) = sides()
    copies = []
    for slot, g in enumerate(chosen):
        members = groups[g]
        sources = [(t, 3 * members[0], 3 * len(members))]
        sources += [(u, 0, 3)] if g == 0 else []
        for side, plane in ((0, z_plane), (1, x_plane)):
            at = 0
            for ref, start, count in sources:
                copies.append(
                    pltpu.make_async_copy(
                        ref.at[pl.ds(start, count), plane],
                        outs[2 * slot + side].at[pl.ds(at, count)],
                        sem.at[len(copies)],
                    )
                )
                at += count
    for copy in copies:
        copy.start()
    for copy in copies:
        copy.wait()


def pack_tile(load, fields, x, packed, even_lane, plane_lane):
    own = jnp.zeros(tile, f32)
    for f in fields:
        own = jnp.where(even_lane == 2 * f, pltpu.roll(load(f), 2 * f + 1, axis=1), own)
    return jnp.where(plane_lane == x, pltpu.roll(own, 32 * x, axis=1), packed)


def lane_parts():
    lane = lanes()
    return lane & -2, lane >> 5


def pack_first_kernel(t, u, face, out):
    parts = lane_parts()

    def at_rows(zt, carry):
        rows = rows_of(zt)
        tangent = flow = jnp.zeros(tile, f32)
        for x in range(4):
            tangent = pack_tile(lambda f: t[f, x, rows], range(15), x, tangent, *parts)
            flow = pack_tile(lambda f: u[f, x, rows], range(6), x, flow, *parts)
        out[0, rows] = tangent
        out[1, rows] = flow
        return carry

    lax.fori_loop(0, 8, at_rows, 0)


class PackedLanes:
    def __init__(self):
        lane = lanes()
        field = (lane & 31) >> 1
        tangent = sum(jnp.where(field >= 3 * k, 1, 0) for k in range(1, 5))
        self.high = (lane & 1) == 0
        self.sign = jnp.where(self.high, f32(-1), f32(1))
        self.tangent = tangent
        self.component = field - 3 * tangent
        self.even = gy_even()

    def from_neighbours(self, inner, outer):
        high = jnp.where(self.even, inner, outer)
        low = jnp.where(self.even, outer, inner)
        return jnp.where(self.high, pltpu.roll(high, 127, axis=1), pltpu.roll(low, 1, axis=1))

    def spread_flow(self, flow, at):
        out = None
        for k in range(5):
            turn = (6 * k - 2 * at) % 128
            moved = pltpu.roll(flow, turn, axis=1) if turn else flow
            out = moved if out is None else jnp.where(self.tangent == k, moved, out)
        return out

    def of_component(self, packed, component):
        out = packed
        for i in range(3):
            if i != component:
                out = jnp.where(self.component == i, pltpu.roll(packed, (2 * (i - component)) % 128, axis=1), out)
        return out

    def column_terms(self, scale, tangent, flow, halo, halo_flow, flow_at):
        flag = jnp.where(self.tangent == 4, f32(scale), f32(0))
        speed = self.of_component(self.spread_flow(flow, flow_at), 1)
        weight = scale * viscosity + (0.5 * scale) * self.sign * speed
        made = (0.5 * scale) * self.sign * self.of_component(tangent, 1) + flag
        return weight * halo + made * self.spread_flow(halo_flow, flow_at)


def edge_part(terms, f, edges):
    return jnp.where(edges, pltpu.roll(terms, (127 - 2 * f) % 128, axis=1), 0.0)


def at_edges():
    lane = lanes()
    return (lane == 0) | (lane == 127)


def fill_padding(padded, count):
    for f in range(count):
        padded[f, 0] = jnp.zeros((80, 128), f32)
        padded[f, 5] = jnp.zeros((80, 128), f32)

        def at_plane(x, carry):
            padded[f, x, 0:8] = jnp.zeros(tile, f32)
            padded[f, x, 72:80] = jnp.zeros(tile, f32)
            return carry

        lax.fori_loop(1, 5, at_plane, 0)


def section(padded, members, scale, base, extra, store):
    lane = lanes()
    not_low = jnp.where(lane == 0, f32(0), f32(1))
    not_high = jnp.where(lane == 127, f32(0), f32(1))
    flow_at = 3 * len(members)

    def at_plane(x, carry):
        for zt in range(8):
            first_row = 8 + 8 * zt
            rows = slice(8 * zt, 8 * zt + 8)

            def stencil(f):
                def load(dx, dz):
                    return padded[f, x + 1 + dx, first_row + dz : first_row + dz + 8]

                centre = load(0, 0)
                up, down = pltpu.roll(centre, 127, axis=1), pltpu.roll(centre, 1, axis=1)
                return centre, load(1, 0), load(-1, 0), up, down, load(0, 1), load(0, -1)

            speed, made, bulk = [], [], []
            for i in range(3):
                flow = list(stencil(flow_at + i))
                flow[3], flow[4] = flow[3] * not_high, flow[4] * not_low
                speed.append(flow[0])
                made.append([(-0.5 * scale) * (flow[1 + 2 * j] - flow[2 + 2 * j]) for j in range(3)])
                if 4 in members:
                    total = flow[1] + flow[2] + flow[3] + flow[4] + flow[5] + flow[6]
                    bulk.append(scale * (total - 6.0 * flow[0]))
            halves = [(0.5 * scale) * u for u in speed]
            ahead = [scale * viscosity - h for h in halves]
            behind = [scale * viscosity + h for h in halves]
            ahead[1], behind[1] = ahead[1] * not_high, behind[1] * not_low
            for n, k in enumerate(members):
                around = [stencil(3 * n + i) for i in range(3)]
                for i in range(3):
                    own = around[i]
                    value = (base - 6.0 * viscosity * scale) * own[0]
                    for j in range(3):
                        value += ahead[j] * own[1 + 2 * j] + behind[j] * own[2 + 2 * j]
                        value += made[i][j] * around[j][0]
                    if k == 4:
                        value += bulk[i]
                    if extra is not None:
                        value += 0.5 * extra[3 * k + i, x, rows]
                    store(3 * n + i, x, rows, value)
        return carry

    lax.fori_loop(0, 4, at_plane, 0)


def first_kernel(t, u, columns, *rest):
    outs, padded = rest[:-1], rest[-1]
    fill_padding(padded, 18)

    def copy_plane(x, carry):
        for f in range(15):
            padded[f, x + 1, 8:72] = t[f, x]
        for i in range(3):
            padded[15 + i, x + 1, 8:72] = u[i, x]
        return carry

    lax.fori_loop(0, 4, copy_plane, 0)
    place = {k: (g, n) for g, members in enumerate(groups) for n, k in enumerate(members)}

    def store(f, x, rows, value):
        g, n = place[f // 3]
        outs[g][3 * n + f % 3, x, rows] = value

    section(padded, range(5), time_step, 1.0, None, store)


def halo_terms(scale, sign, speed, tangent):
    weight = scale * viscosity + (0.5 * scale) * sign * speed
    return weight, [(0.5 * scale) * sign * v + (scale if k == 4 else 0.0) for k, v in tangent]


def first_terms_kernel(columns, inner, outer, terms):
    layout = PackedLanes()
    for zt in range(8):
        rows = slice(8 * zt, 8 * zt + 8)
        halo = [layout.from_neighbours(inner[n, rows], outer[n, rows]) for n in range(2)]
        turned = layout.column_terms(time_step, columns[0, rows], columns[1, rows], halo[0], halo[1], 0)
        for x in range(4):
            terms[x, rows] = pltpu.roll(turned, 128 - 32 * x, axis=1) if x else turned


def first_faces_kernel(g, part, terms, t, u, z_in, x_in, z_flow, x_flow, z_out, x_out):
    members = groups[g]
    flow_at = 3 * len(groups[0])
    edges = at_edges()
    for (plane, sign), got, flow_got, out in zip(sides(), (z_in, x_in), (z_flow, x_flow), (z_out, x_out)):
        if g == 0:
            for i in range(3):
                out[flow_at + i] = u[3 + i, plane]
        for zt in range(8):
            rows = slice(8 * zt, 8 * zt + 8)
            here = terms[plane, rows]
            flow_halo = [flow_got[flow_at + i, rows] for i in range(3)]
            tangent = [(k, t[3 * k, plane, rows]) for k in members]
            weight, made = halo_terms(time_step, sign, u[0, plane, rows], tangent)
            for n, k in enumerate(members):
                for i in range(3):
                    j = 3 * n + i
                    value = part[j, plane, rows] + edge_part(here, 3 * k + i, edges)
                    out[j, rows] = value + weight * got[j, rows] + made[n] * flow_halo[i]


def first_whole_kernel(g, part, terms, z_face, x_face, *refs):
    whole, packed = refs[-2:]
    fields = [3 * k + i for k in groups[g] for i in range(3)]
    edges = at_edges()
    lane_facts = lane_parts()
    (z_plane, _), (x_plane, _) = sides()

    def at_rows(zt, carry):
        rows = rows_of(zt)
        total = jnp.zeros(tile, f32)
        for x in (1, 2):
            values = {}
            for j, f in enumerate(fields):
                values[f] = part[j, x, rows] + edge_part(terms[x, rows], f, edges)
                whole[j, x, rows] = values[f]
            total = pack_tile(lambda f: values[f], fields, x, total, *lane_facts)
        for plane, face in ((z_plane, z_face), (x_plane, x_face)):
            values = {}
            for j, f in enumerate(fields):
                values[f] = face[j, rows]
                whole[j, plane, rows] = values[f]
            total = pack_tile(lambda f: values[f], fields, plane, total, *lane_facts)
        packed[rows] = total + refs[0][rows] if g else total
        return carry

    lax.fori_loop(0, 8, at_rows, 0, unroll=2)


def split_refs(refs, *counts):
    pieces, at = [], 0
    for count in counts:
        pieces.append(refs[at : at + count])
        at += count
    pieces.append(refs[at:])
    return pieces


def second_kernel(g, t, u, first, out, padded):
    members = groups[g]
    count = 3 * len(members)
    fill_padding(padded, count + 3)

    def copy_plane(x, carry):
        for j in range(count):
            padded[j, x + 1, 8:72] = first[j, x]
        for i in range(3):
            padded[count + i, x + 1, 8:72] = u[3 + i, x]
        return carry

    lax.fori_loop(0, 4, copy_plane, 0)

    def store(j, x, rows, value):
        out[j, x, rows] = value

    section(padded, members, 0.5 * time_step, 0.5, t, store)


pairs = [(a, b) for a in range(5) for b in range(a, 5)]


def add_products(sums, rows_now, weighted):
    products = [sums[n] + rows_now[a] * rows_now[b] for n, (a, b) in enumerate(pairs)]
    return products + [sums[15 + k] + weighted[k] for k in range(5)]


def second_terms_kernel(packed, columns, inner_flow, outer_flow, inner, outer, terms):
    layout = PackedLanes()
    for zt in range(8):
        rows = slice(8 * zt, 8 * zt + 8)
        halo = layout.from_neighbours(inner[rows], outer[rows])
        halo_flow = layout.from_neighbours(inner_flow[1, rows], outer_flow[1, rows])
        turned = layout.column_terms(0.5 * time_step, packed[rows], columns[1, rows], halo, halo_flow, 3)
        for x in range(4):
            terms[x, rows] = pltpu.roll(turned, 128 - 32 * x, axis=1) if x else turned


def places():
    return {k: (g, 3 * n) for g, members in enumerate(groups) for n, k in enumerate(members)}


def second_inside_kernel(terms, weight, *refs):
    parts, first, (out, sums_out) = split_refs(refs, len(groups), len(groups))
    edges = at_edges()
    place = places()
    sums = [jnp.zeros(tile, f32)] * 20
    for x in (1, 2):

        def at_rows(zt, sums):
            rows = rows_of(zt)
            here = terms[x, rows]
            for i in range(3):
                now, weighted = [], []
                scaled = weight[i, x, rows]
                for k in range(5):
                    g, j = place[k][0], place[k][1] + i
                    value = parts[g][j, x, rows] + edge_part(here, 3 * k + i, edges)
                    out[3 * k + i, x - 1, rows] = value
                    now.append(value)
                    weighted.append(scaled * (first[g][j, x, rows] + value))
                sums = add_products(sums, now, weighted)
            return sums

        sums = lax.fori_loop(0, 8, at_rows, sums, unroll=4)
    for n in range(20):
        sums_out[n] = sums[n]


def second_outer_kernel(u, weight, terms, sums_in, z_flow, x_flow, *refs):
    count = len(groups)
    parts, first, z_in, x_in, (z_out, x_out, sums_out) = split_refs(refs, count, count, count, count)
    flow_at = 3 * len(groups[0])
    scale = 0.5 * time_step
    edges = at_edges()
    place = places()
    sums = [sums_in[n] for n in range(20)]
    for (plane, sign), got, flow_got, out in zip(sides(), (z_in, x_in), (z_flow, x_flow), (z_out, x_out)):

        def at_rows(zt, sums):
            rows = rows_of(zt)
            here = terms[plane, rows]
            flow_halo = [flow_got[flow_at + i, rows] for i in range(3)]
            tangent = [(k, first[place[k][0]][place[k][1], plane, rows]) for k in range(5)]
            outer_weight, made = halo_terms(scale, sign, u[3, plane, rows], tangent)
            for i in range(3):
                now, weighted = [], []
                scaled = weight[i, plane, rows]
                for k in range(5):
                    g, j = place[k][0], place[k][1] + i
                    value = parts[g][j, plane, rows] + edge_part(here, 3 * k + i, edges)
                    value += outer_weight * got[g][j, rows] + made[k] * flow_halo[i]
                    out[3 * k + i, rows] = value
                    now.append(value)
                    weighted.append(scaled * (first[g][j, plane, rows] + value))
                sums = add_products(sums, now, weighted)
            return sums

        sums = lax.fori_loop(0, 8, at_rows, sums, unroll=4)
    stacked = jnp.concatenate([jnp.sum(s, axis=0, keepdims=True) for s in sums] + [jnp.zeros((4, 128), f32)], 0)
    totals = jnp.broadcast_to(jnp.sum(stacked, axis=1, keepdims=True), (24, 128))
    diagonal = lax.broadcasted_iota(jnp.int32, (24, 128), 0) == lax.broadcasted_iota(jnp.int32, (24, 128), 1)
    line = jnp.sum(jnp.where(diagonal, totals, 0.0), axis=0, keepdims=True)
    sums_out[...] = jnp.broadcast_to(line[None], sums_out.shape)


def renorm_kernel(total_cells, inside, z_face, x_face, gathered, out, r_out, c_out, o_out, ready, sem):
    chains = []
    for first in range(8):
        chain = gathered[first]
        for device in range(first + 8, gathered.shape[0], 8):
            chain = chain + gathered[device]
        chains.append(chain)
    while len(chains) > 1:
        chains = [chains[n] + chains[n + 1] for n in range(0, len(chains), 2)]
    line = chains[0]
    spread = [jnp.broadcast_to(line[:, n : n + 1], tile) for n in range(20)]
    gram = {pair: spread[n] * f32(1.0 / (3.0 * total_cells)) for n, pair in enumerate(pairs)}
    lower, below = {}, {}
    for c in range(4):
        value = gram[(c, c)]
        for m in range(c):
            value = value - lower[(c, m)] * lower[(c, m)]
        lower[(c, c)] = jnp.sqrt(value)
        below[c] = 1.0 / lower[(c, c)]
        for r in range(c + 1, 4):
            value = gram[(c, r)]
            for m in range(c):
                value = value - lower[(r, m)] * lower[(c, m)]
            lower[(r, c)] = value * below[c]
    inverse = {}
    for r in range(4):
        for c in range(r + 1):
            value = jnp.ones(tile, f32) if r == c else jnp.zeros(tile, f32)
            for m in range(c, r):
                value = value - lower[(r, m)] * inverse[(m, c)]
            inverse[(r, c)] = value * below[r]
    coefficient = []
    for r in range(4):
        value = inverse[(r, 0)] * gram[(0, 4)]
        for c in range(1, r + 1):
            value = value + inverse[(r, c)] * gram[(c, 4)]
        coefficient.append(value)

    row, lane = lax.broadcasted_iota(jnp.int32, tile, 0), lanes()
    factor, coefficients, objective = (jnp.zeros(tile, f32) for _ in range(3))
    for r in range(4):
        for c in range(r + 1):
            factor = jnp.where((row == c) & (lane == r), lower[(r, c)], factor)
        coefficients = jnp.where(lane == r, coefficient[r], coefficients)
    for k in range(5):
        objective = jnp.where(lane == k, spread[15 + k] * f32(0.5 / total_cells), objective)
    r_out[...] = factor[:4, :4]
    c_out[...] = coefficients[0, :4]
    o_out[...] = objective[0, :5]

    (z_plane, _), (x_plane, _) = sides()
    copies = []
    for plane, load in (
        (1, lambda f, rows: inside[f, 0, rows]),
        (2, lambda f, rows: inside[f, 1, rows]),
        (z_plane, lambda f, rows: z_face[f, rows]),
        (x_plane, lambda f, rows: x_face[f, rows]),
    ):

        def at_rows(zt, carry):
            rows = rows_of(zt)
            for i in range(3):
                now = [load(3 * k + i, rows) for k in range(5)]
                last = now[4]
                for r in range(4):
                    value = inverse[(r, 0)] * now[0]
                    for c in range(1, r + 1):
                        value = value + inverse[(r, c)] * now[c]
                    ready[3 * r + i, plane, rows] = value
                    last = last - coefficient[r] * value
                ready[12 + i, plane, rows] = last
            return carry

        lax.fori_loop(0, 8, at_rows, 0, unroll=4)
        copy = pltpu.make_async_copy(ready.at[:, plane], out.at[:, plane], sem.at[len(copies)])
        copy.start()
        copies.append(copy)
    for copy in copies:
        copy.wait()


def per_device(tangents, base_flow, objective_weight):
    count_x, count_y = lax.axis_size("gx"), lax.axis_size("gy")
    total_cells = 4 * 64 * 128 * count_x * count_y
    t = tangents.reshape(15, 4, 64, 128)
    u = base_flow.reshape(6, 4, 64, 128)
    last = len(groups) - 1

    def partner(values, axis, count):
        return lax.ppermute(values, axis, [(i, i ^ 1) for i in range(count)])

    def beyond(values, axis, count):
        return lax.ppermute(values, axis, [(i, (i + 2 * (i % 2) - 1) % count) for i in range(count)])

    def after(values, other):
        return lax.optimization_barrier((values, other))[0]

    sizes = [3 * len(members) for members in groups]
    sent = [s + (3 if g == 0 else 0) for g, s in enumerate(sizes)]
    def send_buffers(chosen, limit):
        return pl.pallas_call(
            functools.partial(faces_kernel, chosen),
            out_shape=tuple(shaped(sent[g], 64, 128) for g in chosen for _ in range(2)),
            in_specs=[pl.BlockSpec(memory_space=pltpu.HBM)] * 2,
            out_specs=(vmem,) * (2 * len(chosen)),
            scratch_shapes=[pltpu.SemaphoreType.DMA((2 * len(chosen) + 4,))],
            compiler_params=pltpu.CompilerParams(vmem_limit_bytes=limit),
        )(t, u)

    faces = [*send_buffers((0,), None), *send_buffers(tuple(range(1, len(groups))), 8 << 20)]
    z_in = [partner(faces[0], "gx", count_x)]
    x_in = [beyond(faces[1], "gx", count_x)]
    columns = call(pack_first_kernel, shaped(2, 64, 128), (t, u, faces[1]))
    inner_in = partner(columns, "gy", count_y)
    outer_in = beyond(after(columns, inner_in), "gy", count_y)
    parts = call(
        first_kernel,
        tuple(shaped(s, 4, 64, 128) for s in sizes),
        (t, u, columns),
        scratch=[pltpu.VMEM((18, 6, 80, 128), f32)],
        flops=10000000,
    )
    for g in range(1, len(groups)):
        z_in.append(partner(after(faces[2 * g], inner_in), "gx", count_x))
        x_in.append(beyond(after(faces[2 * g + 1], inner_in), "gx", count_x))
    terms = call(first_terms_kernel, shaped(4, 64, 128), (columns, inner_in, outer_in))
    first, halves, z_next, x_next = [], [], [], []
    packed = ()
    for g in range(len(groups)):
        if g:
            z_in[g] = after(z_in[g], halves[-1])
        z_face, x_face = call(
            functools.partial(first_faces_kernel, g),
            (shaped(sent[g], 64, 128), shaped(sent[g], 64, 128)),
            (parts[g], terms, t, u, z_in[g], x_in[g], z_in[0], x_in[0]),
        )
        z_next.append(partner(z_face, "gx", count_x))
        x_next.append(beyond(x_face, "gx", count_x))
        whole, *packed = call(
            functools.partial(first_whole_kernel, g),
            (shaped(sizes[g], 4, 64, 128), shaped(64, 128)),
            (parts[g], terms, z_face, x_face, *packed),
        )
        first.append(whole)
        halves.append(
            call(
                functools.partial(second_kernel, g),
                shaped(sizes[g], 4, 64, 128),
                (t, u, whole),
                scratch=[pltpu.VMEM((sizes[g] + 3, 6, 80, 128), f32)],
                flops=5000000,
            )
        )
    inner = partner(packed[0], "gy", count_y)
    outer = beyond(after(packed[0], inner), "gy", count_y)
    terms = call(second_terms_kernel, shaped(4, 64, 128), (packed[0], columns, inner_in, outer_in, inner, outer))
    inside, sums = call(
        second_inside_kernel,
        (shaped(15, 2, 64, 128), shaped(20, 8, 128)),
        (terms, objective_weight, *halves, *first),
    )
    z_face, x_face, line = call(
        second_outer_kernel,
        (shaped(15, 64, 128), shaped(15, 64, 128), shaped(count_x * count_y, 1, 128)),
        (u, objective_weight, terms, sums, z_next[0], x_next[0], *halves, *first, *z_next, *x_next),
    )
    gathered = lax.all_to_all(line, ("gx", "gy"), 0, 0, tiled=True)
    renormed, rfactor, coefficients, objective = pl.pallas_call(
        functools.partial(renorm_kernel, total_cells),
        out_shape=(shaped(15, 4, 64, 128), shaped(4, 4), shaped(4), shaped(5)),
        in_specs=[vmem] * 4,
        out_specs=(pl.BlockSpec(memory_space=pl.ANY), vmem, vmem, vmem),
        scratch_shapes=[pltpu.VMEM((15, 4, 64, 128), f32), pltpu.SemaphoreType.DMA((4,))],
        compiler_params=pltpu.CompilerParams(vmem_limit_bytes=24 << 20),
    )(inside, z_face, x_face, gathered)
    return (renormed.reshape(tangents.shape), rfactor, coefficients, objective)


def solution(mesh):
    placed = (
        P(None, None, "gx", None, "gy"),
        P(None, None, "gx", None, "gy"),
        P(None, "gx", None, "gy"),
    )
    return jax.shard_map(
        per_device,
        mesh=mesh,
        in_specs=placed,
        out_specs=(P(None, None, "gx", None, "gy"), P(), P(), P()),
        check_vma=False,
    )
```
